128 devices in a mesh: grp: 4 (over x_hi, core), dev: 32 (over z, y, x_lo).
Axes of the slice: x: 4 (x_hi: 2, x_lo: 2; x = x_hi * 2 + x_lo), y: 4, z: 4, core: 2. Of those that a mesh axis runs over, the one named last changes fastest.
Arguments:
- spin_config: int32 [256, 144], P(('grp', 'dev')), may hold values from -1 to 1, as said below
- layer_acts: bfloat16 [256, 36, 768], P(('grp', 'dev'))
- cotangent: bfloat16 [256, 36, 768], P(('grp', 'dev'))
- patch_embed: bfloat16 [4, 768], replicated, may hold values from -3 to 3
- energies: float32 [256], P(('grp', 'dev')), may hold values from -0.24 to 0.24
- slot_sample: int32 [256], replicated, may hold values from 0 to 255, each once
- damping: float32 [], replicated, may hold values from 0.0001 to 0.0002
Outputs:
- update: float32 [589824], P(('grp', 'dev'))
The draws below stay inside these ranges and needn't reach their ends.
Inputs may be any that keep to these rules, and one draw needn't show every extreme that they name: `spin_config`: each entry is -1 or +1; the sites of patch t are entries 4 t to 4 t + 3.
All inputs are finite; a program needn't handle non-finite values.
Results may differ from the reference program's by a relative error of at most 0.001.
The reference program's roundings to bfloat16 on the way count: a program that leaves them out, or rounds other values in their place, can miss the bound.
Values may be sent and summed in bfloat16 or wider, within the bound.
A program may use at most 64 MiB of HBM per device.

```python
import math
import jax
import jax.numpy as jnp
from jax import lax

D = 768
SITES = 144
PATCH = 4
TOKS = 36
SAMPLES = 256
PARAMS = 589824


floor_level = 2e-05


left_terms = 44


right_terms = 48


def decay_step():
    return math.log(1.0 / floor_level) / (2.0 * SAMPLES)


def combine(coeffs, patterns, rates):

    def add_term(index, total):
        column = lax.dynamic_slice_in_dim(coeffs, index, 1, 2)
        pattern = lax.dynamic_slice_in_dim(patterns, index, 1, 0)
        rate = lax.dynamic_slice_in_dim(rates, index, 1, 0)
        return total + column * (rate[0] * pattern)
    start = jnp.zeros((coeffs.shape[0], coeffs.shape[1], patterns.shape[1]), jnp.float32)
    return lax.fori_loop(0, coeffs.shape[2], add_term, start)


def draw_spin_config(key, part):
    key = jax.random.fold_in(key, 5)
    return 2 * jax.random.randint(key, (SAMPLES, SITES), 0, 2, jnp.int32) - 1


def draw_layer_acts(key, part):
    key = jax.random.fold_in(key, 11)
    coeff_key, pattern_key, jitter_key = jax.random.split(key, 3)
    coeff_shape = (SAMPLES, TOKS, left_terms)
    coeffs = jax.random.normal(coeff_key, coeff_shape, jnp.float32)
    patterns = jax.random.normal(pattern_key, (left_terms, D), jnp.float32)
    offsets = jax.random.uniform(jitter_key, (left_terms,), jnp.float32, -0.2, 0.2)
    levels = jnp.arange(left_terms, dtype=jnp.float32) + offsets
    rates = jnp.exp(-decay_step() * right_terms * levels)
    return combine(coeffs, patterns, rates).astype(jnp.bfloat16)


def draw_cotangent(key, part):
    key = jax.random.fold_in(key, 23)
    coeff_key, pattern_key, jitter_key = jax.random.split(key, 3)
    coeff_shape = (SAMPLES, TOKS, right_terms)
    coeffs = jax.random.normal(coeff_key, coeff_shape, jnp.float32)
    patterns = jax.random.normal(pattern_key, (right_terms, D), jnp.float32)
    offsets = jax.random.uniform(jitter_key, (right_terms,), jnp.float32, -0.4, 0.4)
    levels = jnp.arange(right_terms, dtype=jnp.float32) + offsets
    rates = jnp.exp(-decay_step() * levels) * (1.0 / math.sqrt(SAMPLES))
    return combine(coeffs, patterns, rates).astype(jnp.bfloat16)


def level_of(key, shape, cuts, least, high):
    def one(position, shards_of):
        heights = jax.random.uniform(jax.random.fold_in(jax.random.fold_in(key, 6), position), (shards_of,), jnp.float32, least / len(cuts), high / len(cuts))
        return jnp.repeat(jnp.exp(heights), shape[position] // shards_of).reshape((-1,) + (1,) * (len(shape) - position - 1))

    loudness = one(*cuts[0])
    for cut in cuts[1:]:
        loudness = loudness * one(*cut)
    return loudness


def centred(rng, dims, width, limit, cuts=(), kind=jnp.bfloat16):
    values = width * jax.random.normal(rng, dims, jnp.float32)
    if cuts:
        values = values * level_of(rng, dims, cuts, -0.22, 0.18)
    return jnp.clip(values, -limit, limit).astype(kind)


def setup_inputs(seed: int = 0) -> dict:
    arg_keys = jax.random.split(jax.random.key(seed), 8)
    spin_config = draw_spin_config(jax.random.fold_in(arg_keys[7], 71), 0)
    layer_acts = draw_layer_acts(jax.random.fold_in(arg_keys[7], 71), 0)
    cotangent = draw_cotangent(jax.random.fold_in(arg_keys[7], 71), 0)
    patch_embed = centred(arg_keys[3], (PATCH, D), 0.5, 3.0)
    energies = centred(arg_keys[4], (SAMPLES,), 0.04, 0.24, ((0, 128),), jnp.float32)
    slot_sample = jax.random.permutation(arg_keys[5], SAMPLES).astype(jnp.int32)
    damping = jnp.clip(jnp.exp(jax.random.uniform(arg_keys[6], (), jnp.float32, math.log(0.0001), math.log(0.0002))), 0.0001, 0.0002)
    return dict(spin_config=spin_config, layer_acts=layer_acts, cotangent=cotangent, patch_embed=patch_embed, energies=energies, slot_sample=slot_sample, damping=damping)


def layer_inputs(spin_config, layer_acts, patch_embed):
    patches = spin_config.reshape(spin_config.shape[0], layer_acts.shape[1], -1).astype(jnp.float32)
    embedded = jnp.einsum('stk,kd->std', patches, patch_embed.astype(jnp.float32))
    return (layer_acts.astype(jnp.float32) + embedded).astype(jnp.bfloat16)

def solve_system(system, target):
    factor = jnp.linalg.cholesky(system)
    forward = lax.linalg.triangular_solve(factor, target[:, None], left_side=True, lower=True)
    backward = lax.linalg.triangular_solve(factor, forward, left_side=True, lower=True, transpose_a=True)
    return backward[:, 0]

def reference(spin_config, layer_acts, cotangent, patch_embed, energies, slot_sample, damping):
    layer_in = layer_inputs(spin_config, layer_acts, patch_embed)
    stride = math.gcd(D, 8)
    blocks_total = D // stride
    inv_root = 1.0 / math.sqrt(PARAMS)
    tok_scale = 1.0 / math.sqrt(TOKS)
    left_all = layer_in.astype(jnp.float32)
    right_all = cotangent.astype(jnp.float32)

    def centered_block(block_index):
        left_in = lax.dynamic_slice_in_dim(left_all, (block_index * stride).astype(jnp.int32), stride, 2)
        row_block = (jnp.einsum('sti,stj->sij', left_in, right_all) * tok_scale).astype(jnp.bfloat16)
        row_block = row_block.reshape(SAMPLES, stride * D).astype(jnp.float32)
        return ((row_block - lax.optimization_barrier(jnp.mean(row_block, axis=0, keepdims=True))) * inv_root).astype(jnp.bfloat16)

    def add_block(running, block_index):
        col_block = centered_block(block_index).astype(jnp.float32)
        return (running + jnp.dot(col_block, col_block.T, precision=lax.Precision.HIGHEST), None)
    gram_matrix, unused = lax.scan(add_block, jnp.zeros((SAMPLES, SAMPLES), jnp.float32), jnp.arange(blocks_total, dtype=jnp.int32))
    shifted = jnp.take(energies, slot_sample) - jnp.mean(energies)
    system = gram_matrix + damping * jnp.eye(SAMPLES, dtype=jnp.float32)
    weights = solve_system(system, shifted)
    step_scale = -math.sqrt(PARAMS / SAMPLES)

    def update_block(block_index):
        col_block = centered_block(block_index).astype(jnp.float32)
        return step_scale * jnp.dot(weights, col_block, precision=lax.Precision.HIGHEST)
    update = lax.map(update_block, jnp.arange(blocks_total, dtype=jnp.int32))
    return update.reshape(PARAMS)
```

```python
import math

import jax
import jax.numpy as jnp
from jax import lax
from jax.experimental import pallas as pl
from jax.experimental.pallas import tpu as pltpu
from jax.sharding import PartitionSpec as P

F32 = jnp.float32
BF = jnp.bfloat16
MESH = pl.DeviceIdType.MESH
SLOTS = 256
WIDTH = 768
TOKS = 36
IB = 48
JB = 96
ROWS2 = 2 * TOKS
LANES = 128


def flip(index, high):
    return index + high * (1 - 2 * (index % 2))


def place():
    g = lax.axis_index("grp")
    d = lax.axis_index("dev")
    x_hi, core = g // 2, g % 2
    z, rb = d // 8, d % 8
    return g, d, x_hi, core, z, rb


def column_device(a, b):
    g, z = a // 4, a % 4
    return (g, z * 8 + flip(b, g // 2))


def remote(src, dst, send_sem, recv_sem, device):
    return pltpu.make_async_remote_copy(
        src_ref=src, dst_ref=dst, send_sem=send_sem, recv_sem=recv_sem,
        device_id=device, device_id_type=MESH,
    )


def gram_kernel(energy_ref, lin_ref, cin_ref, slot_ref, out_ref, cen_ref,
                lall, call, rbuf, gacc, gp, rr, ssum, cr, tile, s2,
                l1s, l1r, c1s, c1r, c2s, c2r, c3s, c3r, l2s, l2r,
                rs_s, rs_r, cs_s, cs_r, bc_s, bc_r, ag_s, ag_r):
    g, d, x_hi, core, z, rb = place()
    a = g * 4 + z
    b = flip(rb, x_hi)
    chip = x_hi * 4 + z
    partner = (x_hi * 2 + 1 - core, d)

    barrier = pltpu.get_barrier_semaphore()
    for k in range(1, 16):
        pl.semaphore_signal(barrier, inc=1, device_id=column_device((a + k) % 16, b), device_id_type=MESH)
    for k in range(1, 8):
        pl.semaphore_signal(barrier, inc=1, device_id=column_device(a, (b + k) % 8), device_id_type=MESH)
    pl.semaphore_wait(barrier, 22)

    sends = []

    def start(copy):
        copy.start()
        sends.append(copy)

    for k in range(1, 8):
        bt = (b + k) % 8
        start(remote(cin_ref.at[bt], call.at[a, b], c1s.at[k], c1r.at[b], column_device(a, bt)))
    for k in range(1, 16):
        at = (a + k) % 16
        start(remote(lin_ref.at[at], lall.at[b, a], l1s.at[k], l1r.at[a], column_device(at, b)))
    call[a, b] = cin_ref[b]
    lall[b, a] = lin_ref[a]

    for k in range(1, 8):
        bs = (b + 8 - k) % 8
        remote(call.at[a, bs], call.at[a, bs], c1s.at[k], c1r.at[bs], partner).wait_recv()
    for k in range(1, 8):
        ct = (chip + k) % 8
        at = (ct // 4) * 8 + core * 4 + ct % 4
        start(remote(call.at[a], call.at[a], c2s.at[k], c2r.at[chip], column_device(at, b)))
    start(remote(call.at[a], call.at[a], c3s.at[0], c3r.at[chip], partner))

    for k in range(1, 16):
        asrc = (a + 16 - k) % 16
        remote(lall.at[b, asrc], lall.at[b, asrc], l1s.at[k], l1r.at[asrc], partner).wait_recv()
    for k in range(1, 8):
        bt = (b + k) % 8
        start(remote(lall.at[b], lall.at[b], l2s.at[k], l2r.at[b], column_device(a, bt)))

    for k in range(1, 8):
        cs = (chip + 8 - k) % 8
        asrc = (cs // 4) * 8 + core * 4 + cs % 4
        remote(call.at[asrc], call.at[asrc], c2s.at[k], c2r.at[cs], partner).wait_recv()
        start(remote(call.at[asrc], call.at[asrc], c3s.at[k], c3r.at[cs], partner))
    for k in range(0, 8):
        cs = (chip + 8 - k) % 8
        asrc = (cs // 4) * 8 + (1 - core) * 4 + cs % 4
        remote(call.at[asrc], call.at[asrc], c3s.at[k], c3r.at[cs], partner).wait_recv()
    for k in range(1, 8):
        bs = (b + 8 - k) % 8
        remote(lall.at[bs], lall.at[bs], l2s.at[k], l2r.at[bs], partner).wait_recv()

    lane = lax.broadcasted_iota(jnp.int32, (IB, LANES), 1)
    first = jnp.where(lane < TOKS, 1.0, 0.0).astype(BF)
    second = jnp.where((lane >= TOKS) & (lane < ROWS2), 1.0, 0.0).astype(BF)

    def rows_step(asrc, carry):
        high = asrc // 8
        for bs in range(8):
            left = lall[bs, asrc]
            left = jnp.concatenate([left * first, left * second], axis=0)
            prod = lax.dot_general(left[:, :ROWS2], call[asrc, bs], (((1,), (0,)), ((), ())),
                                   preferred_element_type=F32)
            at = asrc * 8 + flip(bs, high)
            rbuf[pl.ds(pl.multiple_of(at * 2 * IB, 2 * IB), 2 * IB), :] = (
                prod * (1.0 / math.sqrt(TOKS))).astype(BF).astype(F32)
        return carry

    lax.fori_loop(0, 16, rows_step, 0)

    gacc[...] = jnp.zeros_like(gacc)
    inv_root = 1.0 / math.sqrt(WIDTH * WIDTH)

    def gram_step(step, carry):
        parts = []
        for u in range(4):
            i = step * 4 + u
            x = rbuf[pl.ds(i, SLOTS, stride=IB), :]
            mean = jnp.sum(x, axis=0, keepdims=True) * (1.0 / SLOTS)
            c = ((x - mean) * inv_root).astype(BF)
            cen_ref[i] = c
            parts.append(c)
        c = jnp.concatenate(parts, axis=1)
        gacc[...] += lax.dot_general(c, c, (((1,), (1,)), ((), ())), preferred_element_type=F32)
        return carry

    lax.fori_loop(0, IB // 4, gram_step, 0)

    for t in range(48):
        blk, w = t // 16, t % 16
        r0 = (0, 128, 128)[blk] + 8 * w
        c0 = (0, 0, 128)[blk]
        gp[t // 6, t % 6] = gacc[r0:r0 + 8, c0:c0 + 128]
    slots = slot_ref[...]
    base = (g * 32 + d) * 2
    mine = jnp.where(slots == base, energy_ref[0, 0], 0.0) + jnp.where(slots == base + 1, energy_ref[0, 1], 0.0)
    for r in range(8):
        gp[r, 6] = mine if r == 0 else jnp.zeros_like(mine)

    for k in range(1, 8):
        bt = (b + k) % 8
        start(remote(gp.at[bt], rr.at[b], rs_s.at[k], rs_r.at[b], column_device(a, bt)))
    for k in range(1, 8):
        bs = (b + 8 - k) % 8
        remote(rr.at[bs], rr.at[bs], rs_s.at[k], rs_r.at[bs], partner).wait_recv()
    rr[b] = gp[b]
    total = rr[0]
    for k in range(1, 8):
        total = total + rr[k]
    ssum[...] = total

    for j in range(7):
        owner = (j % 2) * 8 + j // 2

        @pl.when(a != owner)
        def _():
            remote(ssum.at[j], cr.at[a], cs_s.at[j], cs_r.at[a], column_device(owner + 0 * a, b)).start()

    for j in range(7):
        owner = (j % 2) * 8 + j // 2

        @pl.when(a == owner)
        def _():
            for k in range(1, 16):
                asrc = (a + k) % 16
                remote(cr.at[asrc], cr.at[asrc], cs_s.at[j], cs_r.at[asrc], partner).wait_recv()
            cr[owner] = ssum[j]
            t = cr[0]
            for k in range(1, 16):
                t = t + cr[k]
            s2[j] = t
            for k in range(1, 16):
                at = (a + k) % 16
                remote(s2.at[j], s2.at[j], bc_s.at[k], bc_r.at[j], column_device(at, b)).start()

    for j in range(7):
        owner = (j % 2) * 8 + j // 2

        @pl.when(a != owner)
        def _():
            remote(ssum.at[j], cr.at[a], cs_s.at[j], cs_r.at[a], partner).wait_send()
            remote(s2.at[j], s2.at[j], bc_s.at[0], bc_r.at[j], partner).wait_recv()

    for k in range(1, 8):
        bt = (b + k) % 8
        start(remote(s2, out_ref.at[b], ag_s.at[k], ag_r.at[b], column_device(a, bt)))
    out_ref[b] = s2[...]
    for k in range(1, 8):
        bs = (b + 8 - k) % 8
        remote(out_ref.at[bs], out_ref.at[bs], ag_s.at[k], ag_r.at[bs], partner).wait_recv()

    for copy in sends:
        copy.wait_send()
    for j in range(7):
        owner = (j % 2) * 8 + j // 2

        @pl.when(a == owner)
        def _():
            for k in range(1, 16):
                remote(s2.at[j], s2.at[j], bc_s.at[k], bc_r.at[j], partner).wait_send()


def gram_call(energy, lin, cin, slots):
    dma = pltpu.SemaphoreType.DMA
    vmem = pl.BlockSpec(memory_space=pltpu.VMEM)
    return pl.pallas_call(
        gram_kernel,
        out_shape=(
            jax.ShapeDtypeStruct((8, 7, 8, LANES), F32),
            jax.ShapeDtypeStruct((IB, SLOTS, LANES), BF),
        ),
        in_specs=[pl.BlockSpec(memory_space=pltpu.SMEM), vmem, vmem, vmem],
        out_specs=(vmem, vmem),
        scratch_shapes=[
            pltpu.VMEM((8, 16, IB, LANES), BF),
            pltpu.VMEM((16, 8, ROWS2, LANES), BF),
            pltpu.VMEM((SLOTS * IB, LANES), F32),
            pltpu.VMEM((SLOTS, SLOTS), F32),
            pltpu.VMEM((8, 7, 8, LANES), F32),
            pltpu.VMEM((8, 7, 8, LANES), F32),
            pltpu.VMEM((7, 8, LANES), F32),
            pltpu.VMEM((16, 8, LANES), F32),
            pltpu.VMEM((8, LANES), F32),
            pltpu.VMEM((7, 8, LANES), F32),
            dma((16,)), dma((16,)), dma((8,)), dma((8,)), dma((8,)), dma((8,)),
            dma((8,)), dma((8,)), dma((8,)), dma((8,)),
            dma((8,)), dma((8,)), dma((8,)), dma((16,)), dma((16,)), dma((8,)), dma((8,)), dma((8,)),
        ],
        compiler_params=pltpu.CompilerParams(
            collective_id=0, has_side_effects=True, vmem_limit_bytes=48 * 1024 * 1024),
        name="gram",
    )(energy, lin, cin, slots)


def split3(x):
    high = x.astype(BF)
    rest = x - high.astype(F32)
    mid = rest.astype(BF)
    return high, mid, (rest - mid.astype(F32)).astype(BF)


def solve_kernel(damp_ref, gt_ref, w_ref, W):
    n, B = SLOTS, 8
    for t in range(48):
        blk, w = t // 16, t % 16
        r0 = (0, 128, 128)[blk] + 8 * w
        c0 = (0, 0, 128)[blk]
        W[r0:r0 + 8, c0:c0 + 128] = gt_ref[t // 6, t % 6]
    W[0:128, 128:256] = W[128:256, 0:128].T
    energy = gt_ref[0, 6]
    e_row = jnp.concatenate([energy[0:1, :], energy[1:2, :]], axis=1)
    sh = e_row - jnp.sum(e_row, axis=1, keepdims=True) * (1.0 / n)
    rows = lax.broadcasted_iota(jnp.int32, (n, n), 0)
    cols = lax.broadcasted_iota(jnp.int32, (n, n), 1)
    eye = rows == cols
    W[:, 0:n] = W[:, 0:n] + jnp.where(eye, damp_ref[0, 0], 0.0)
    W[:, n:] = jnp.broadcast_to(jnp.sum(jnp.where(eye, sh, 0.0), axis=1, keepdims=True), (n, LANES))

    lane128 = lax.broadcasted_iota(jnp.int32, (B, LANES), 1)
    sub128 = lax.broadcasted_iota(jnp.int32, (B, LANES), 0)
    laneN = lax.broadcasted_iota(jnp.int32, (B, n + LANES), 1)
    subN = lax.broadcasted_iota(jnp.int32, (B, n + LANES), 0)

    def chain(k, p):
        dd = pltpu.roll(p[:, 0:n], n - B * k, 1)[:, 0:LANES]
        dd = jnp.where(lane128 < B, dd, jnp.where(lane128 == sub128 + B, 1.0, 0.0))
        for i in range(B):
            c = jnp.broadcast_to(dd[:, i:i + 1], (B, LANES))
            inv = 1.0 / c[i:i + 1, :]
            cm = jnp.where(sub128 == i, 0.0, c)
            r_d = dd[i:i + 1, :] * inv
            dd = jnp.where(sub128 == i, r_d, dd - cm * r_d)
            r_p = p[i:i + 1, :] * jnp.concatenate([inv] * 3, axis=1)
            p = jnp.where(subN == i, r_p, p - jnp.concatenate([cm] * 3, axis=1) * r_p)
        dinv = jnp.concatenate([dd, jnp.zeros((B, n - LANES), F32)], axis=1)
        dinv = pltpu.roll(dinv, lax.rem(B * k - B + n, n), 1)
        dinv = jnp.concatenate([dinv, jnp.zeros((B, LANES), F32)], axis=1)
        inside = (laneN >= B * k) & (laneN < B * k + B)
        ident = jnp.where(laneN == B * k + subN, 1.0, 0.0)
        return jnp.where(inside, ident - dinv, p), jnp.where(inside, -dinv, p)

    def stack(p, x):
        ph, pm, pl_ = split3(p)
        xh, xm, xl = split3(x)
        join = lambda *parts: jnp.concatenate([q.astype(F32) for q in parts], axis=0).astype(BF)
        return join(ph, ph, pm, ph, pl_, pm), join(xh, xm, xh, xl, xh, xm)

    def body(k, carry):
        p, p_old, x_old, xs_old = carry
        ps, xs = stack(p_old[:, 0:n], x_old)
        W[...] = W[...] - lax.dot_general(ps, xs, (((0,), (0,)), ((), ())), preferred_element_type=F32)
        kp = pl.multiple_of(jnp.maximum(k - 1, 0) * B, B)
        W[pl.ds(kp, B), :] = jnp.where(k > 0, xs_old, W[pl.ds(kp, B), :])
        x_new, xs_new = chain(k, p)
        kn = pl.multiple_of(jnp.minimum(k + 1, n // B - 1) * B, B)
        nxt = W[pl.ds(kn, B), :]
        col = pltpu.roll(nxt[:, 0:n], n - B * k, 1)
        for i in range(B):
            nxt = nxt - col[:, i:i + 1] * x_new[i:i + 1, :]
        return nxt, p, x_new, xs_new

    zero = jnp.zeros((B, n + LANES), F32)
    _, p_old, x_old, xs_old = lax.fori_loop(0, n // B, body, (W[0:B, :], zero, zero, zero))
    ps, xs = stack(p_old[:, 0:n], x_old)
    w_ref[...] = W[:, n:] - lax.dot_general(ps, xs[:, n:], (((0,), (0,)), ((), ())), preferred_element_type=F32)
    w_ref[n - B:, :] = xs_old[:, n:]


def solve_call(damping, tiles):
    vmem = pl.BlockSpec(memory_space=pltpu.VMEM)
    return pl.pallas_call(
        solve_kernel,
        out_shape=jax.ShapeDtypeStruct((SLOTS, LANES), F32),
        in_specs=[pl.BlockSpec(memory_space=pltpu.SMEM), vmem],
        out_specs=vmem,
        scratch_shapes=[pltpu.VMEM((SLOTS, SLOTS + LANES), F32)],
        name="solve",
    )(damping, tiles)


def update_kernel(w_ref, cen_ref, out_ref, u, send, recv):
    g, d, x_hi, core, z, rb = place()
    a = g * 4 + z
    b = flip(rb, x_hi)
    barrier = pltpu.get_barrier_semaphore()
    for k in range(1, 8):
        pl.semaphore_signal(barrier, inc=1, device_id=column_device(a, (b + k) % 8), device_id_type=MESH)

    scale = -math.sqrt(WIDTH * WIDTH / SLOTS)

    def step(r, carry):
        rows = []
        for v in range(6):
            c = cen_ref[r * 6 + v].astype(F32)
            rows.append(jnp.sum(c * w_ref[...], axis=0, keepdims=True) * scale)
        rows.append(jnp.zeros((2, LANES), F32))
        u[r] = jnp.concatenate(rows, axis=0)
        return carry

    lax.fori_loop(0, 8, step, 0)
    pl.semaphore_wait(barrier, 7)
    sends = []
    for k in range(1, 8):
        rt = (rb + k) % 8
        copy = remote(u.at[rt], out_ref.at[b], send.at[k], recv.at[b], (g, z * 8 + rt))
        copy.start()
        sends.append(copy)
    out_ref[b] = u[rb]
    for k in range(1, 8):
        bs = (b + 8 - k) % 8
        remote(out_ref.at[bs], out_ref.at[bs], send.at[k], recv.at[bs], (g, d)).wait_recv()
    for copy in sends:
        copy.wait_send()


def update_call(weights, cen):
    vmem = pl.BlockSpec(memory_space=pltpu.VMEM)
    return pl.pallas_call(
        update_kernel,
        out_shape=jax.ShapeDtypeStruct((8, 8, LANES), F32),
        in_specs=[vmem, vmem],
        out_specs=vmem,
        scratch_shapes=[pltpu.VMEM((8, 8, LANES), F32), pltpu.SemaphoreType.DMA((8,)), pltpu.SemaphoreType.DMA((8,))],
        compiler_params=pltpu.CompilerParams(
            collective_id=1, has_side_effects=True, vmem_limit_bytes=32 * 1024 * 1024),
        name="update",
    )(weights, cen)


def shards(spin_config, layer_acts, cotangent, patch_embed, energies, slot_sample, damping):
    patches = spin_config.reshape(2, TOKS, -1).astype(F32)
    embedded = jnp.einsum("stk,kd->std", patches, patch_embed.astype(F32))
    layer_in = (layer_acts.astype(F32) + embedded).astype(BF)
    lin = jnp.pad(layer_in.reshape(ROWS2, WIDTH).T, ((0, 0), (0, LANES - ROWS2))).reshape(16, IB, LANES)
    cin = jnp.pad(cotangent.reshape(ROWS2, 8, JB), ((0, 0), (0, 0), (0, LANES - JB))).transpose(1, 0, 2)
    slots = jnp.pad(slot_sample.reshape(2, LANES), ((0, 6), (0, 0)), constant_values=-1)
    tiles, cen = gram_call(energies.reshape(1, 2), lin, cin, slots)
    weights = solve_call(damping.reshape(1, 1), tiles)
    pieces = update_call(weights, cen)
    return pieces[:, :6, :JB].transpose(1, 0, 2).reshape(-1)


def solution(mesh):
    return jax.shard_map(
        shards,
        mesh=mesh,
        in_specs=(
            P(("grp", "dev"), None),
            P(("grp", "dev"), None, None),
            P(("grp", "dev"), None, None),
            P(),
            P(("grp", "dev")),
            P(),
            P(),
        ),
        out_specs=P(("grp", "dev")),
        check_vma=False,
    )
```

```python
import math

import jax
import jax.numpy as jnp
from jax import lax
from jax.experimental import pallas as pl
from jax.experimental.pallas import tpu as pltpu
from jax.sharding import PartitionSpec as P

F32 = jnp.float32
BF = jnp.bfloat16
MESH = pl.DeviceIdType.MESH
SLOTS = 256
WIDTH = 768
TOKS = 36
IB = 48
JB = 96
ROWS2 = 2 * TOKS
LANES = 128


def flip(index, high):
    return index + high * (1 - 2 * (index % 2))


def place():
    g = lax.axis_index("grp")
    d = lax.axis_index("dev")
    x_hi, core = g // 2, g % 2
    z, rb = d // 8, d % 8
    return g, d, x_hi, core, z, rb


def column_device(a, b):
    g, z = a // 4, a % 4
    return (g, z * 8 + flip(b, g // 2))


def remote(src, dst, send_sem, recv_sem, device):
    return pltpu.make_async_remote_copy(
        src_ref=src, dst_ref=dst, send_sem=send_sem, recv_sem=recv_sem,
        device_id=device, device_id_type=MESH,
    )


def gram_kernel(energy_ref, lin_ref, cin_ref, slot_ref, out_ref, cen_ref,
                lall, call, rbuf, gacc, gp, rr, ssum, cr, tile, s2,
                l1s, l1r, c1s, c1r, c2s, c2r, c3s, c3r, l2s, l2r,
                rs_s, rs_r, cs_s, cs_r, bc_s, bc_r, ag_s, ag_r):
    g, d, x_hi, core, z, rb = place()
    a = g * 4 + z
    b = flip(rb, x_hi)
    chip = x_hi * 4 + z
    partner = (x_hi * 2 + 1 - core, d)

    barrier = pltpu.get_barrier_semaphore()
    for k in range(1, 16):
        pl.semaphore_signal(barrier, inc=1, device_id=column_device((a + k) % 16, b), device_id_type=MESH)
    for k in range(1, 8):
        pl.semaphore_signal(barrier, inc=1, device_id=column_device(a, (b + k) % 8), device_id_type=MESH)
    pl.semaphore_wait(barrier, 22)

    sends = []

    def start(copy):
        copy.start()
        sends.append(copy)

    for k in range(1, 8):
        bt = (b + k) % 8
        start(remote(cin_ref.at[bt], call.at[a, b], c1s.at[k], c1r.at[b], column_device(a, bt)))
    for k in range(1, 16):
        at = (a + k) % 16
        start(remote(lin_ref.at[at], lall.at[b, a], l1s.at[k], l1r.at[a], column_device(at, b)))
    call[a, b] = cin_ref[b]
    lall[b, a] = lin_ref[a]

    for k in range(1, 8):
        bs = (b + 8 - k) % 8
        remote(call.at[a, bs], call.at[a, bs], c1s.at[k], c1r.at[bs], partner).wait_recv()
    for k in range(1, 8):
        ct = (chip + k) % 8
        at = (ct // 4) * 8 + core * 4 + ct % 4
        start(remote(call.at[a], call.at[a], c2s.at[k], c2r.at[chip], column_device(at, b)))
    start(remote(call.at[a], call.at[a], c3s.at[0], c3r.at[chip], partner))

    for k in range(1, 16):
        asrc = (a + 16 - k) % 16
        remote(lall.at[b, asrc], lall.at[b, asrc], l1s.at[k], l1r.at[asrc], partner).wait_recv()
    for k in range(1, 8):
        bt = (b + k) % 8
        start(remote(lall.at[b], lall.at[b], l2s.at[k], l2r.at[b], column_device(a, bt)))

    for k in range(1, 8):
        cs = (chip + 8 - k) % 8
        asrc = (cs // 4) * 8 + core * 4 + cs % 4
        remote(call.at[asrc], call.at[asrc], c2s.at[k], c2r.at[cs], partner).wait_recv()
        start(remote(call.at[asrc], call.at[asrc], c3s.at[k], c3r.at[cs], partner))
    for k in range(0, 8):
        cs = (chip + 8 - k) % 8
        asrc = (cs // 4) * 8 + (1 - core) * 4 + cs % 4
        remote(call.at[asrc], call.at[asrc], c3s.at[k], c3r.at[cs], partner).wait_recv()
    for k in range(1, 8):
        bs = (b + 8 - k) % 8
        remote(lall.at[bs], lall.at[bs], l2s.at[k], l2r.at[bs], partner).wait_recv()

    lane = lax.broadcasted_iota(jnp.int32, (IB, LANES), 1)
    first = jnp.where(lane < TOKS, 1.0, 0.0).astype(BF)
    second = jnp.where((lane >= TOKS) & (lane < ROWS2), 1.0, 0.0).astype(BF)

    def rows_step(asrc, carry):
        high = asrc // 8
        for bs in range(8):
            left = lall[bs, asrc]
            left = jnp.concatenate([left * first, left * second], axis=0)
            prod = lax.dot_general(left[:, :ROWS2], call[asrc, bs], (((1,), (0,)), ((), ())),
                                   preferred_element_type=F32)
            at = asrc * 8 + flip(bs, high)
            rbuf[pl.ds(pl.multiple_of(at * 2 * IB, 2 * IB), 2 * IB), :] = (
                prod * (1.0 / math.sqrt(TOKS))).astype(BF).astype(F32)
        return carry

    lax.fori_loop(0, 16, rows_step, 0)

    gacc[...] = jnp.zeros_like(gacc)
    inv_root = 1.0 / math.sqrt(WIDTH * WIDTH)

    def gram_step(step, carry):
        parts = []
        for u in range(4):
            i = step * 4 + u
            x = rbuf[pl.ds(i, SLOTS, stride=IB), :]
            mean = jnp.sum(x, axis=0, keepdims=True) * (1.0 / SLOTS)
            c = ((x - mean) * inv_root).astype(BF)
            cen_ref[i] = c
            parts.append(c)
        c = jnp.concatenate(parts, axis=1)
        gacc[...] += lax.dot_general(c, c, (((1,), (1,)), ((), ())), preferred_element_type=F32)
        return carry

    lax.fori_loop(0, IB // 4, gram_step, 0)

    for t in range(48):
        blk, w = t // 16, t % 16
        r0 = (0, 128, 128)[blk] + 8 * w
        c0 = (0, 0, 128)[blk]
        gp[t // 6, t % 6] = gacc[r0:r0 + 8, c0:c0 + 128]
    slots = slot_ref[...]
    base = (g * 32 + d) * 2
    mine = jnp.where(slots == base, energy_ref[0, 0], 0.0) + jnp.where(slots == base + 1, energy_ref[0, 1], 0.0)
    for r in range(8):
        gp[r, 6] = mine if r == 0 else jnp.zeros_like(mine)

    for k in range(1, 8):
        bt = (b + k) % 8
        start(remote(gp.at[bt], rr.at[b], rs_s.at[k], rs_r.at[b], column_device(a, bt)))
    for k in range(1, 8):
        bs = (b + 8 - k) % 8
        remote(rr.at[bs], rr.at[bs], rs_s.at[k], rs_r.at[bs], partner).wait_recv()
    rr[b] = gp[b]
    total = rr[0]
    for k in range(1, 8):
        total = total + rr[k]
    ssum[...] = total

    for j in range(7):
        owner = (j % 2) * 8 + j // 2

        @pl.when(a != owner)
        def _():
            remote(ssum.at[j], cr.at[a], cs_s.at[j], cs_r.at[a], column_device(owner + 0 * a, b)).start()

    for j in range(7):
        owner = (j % 2) * 8 + j // 2

        @pl.when(a == owner)
        def _():
            for k in range(1, 16):
                asrc = (a + k) % 16
                remote(cr.at[asrc], cr.at[asrc], cs_s.at[j], cs_r.at[asrc], partner).wait_recv()
            cr[owner] = ssum[j]
            t = cr[0]
            for k in range(1, 16):
                t = t + cr[k]
            s2[j] = t
            for k in range(1, 16):
                at = (a + k) % 16
                remote(s2.at[j], s2.at[j], bc_s.at[k], bc_r.at[j], column_device(at, b)).start()

    for j in range(7):
        owner = (j % 2) * 8 + j // 2

        @pl.when(a != owner)
        def _():
            remote(ssum.at[j], cr.at[a], cs_s.at[j], cs_r.at[a], partner).wait_send()
            remote(s2.at[j], s2.at[j], bc_s.at[0], bc_r.at[j], partner).wait_recv()

    for k in range(1, 8):
        bt = (b + k) % 8
        start(remote(s2, out_ref.at[b], ag_s.at[k], ag_r.at[b], column_device(a, bt)))
    out_ref[b] = s2[...]
    for k in range(1, 8):
        bs = (b + 8 - k) % 8
        remote(out_ref.at[bs], out_ref.at[bs], ag_s.at[k], ag_r.at[bs], partner).wait_recv()

    for copy in sends:
        copy.wait_send()
    for j in range(7):
        owner = (j % 2) * 8 + j // 2

        @pl.when(a == owner)
        def _():
            for k in range(1, 16):
                remote(s2.at[j], s2.at[j], bc_s.at[k], bc_r.at[j], partner).wait_send()


def gram_call(energy, lin, cin, slots):
    dma = pltpu.SemaphoreType.DMA
    vmem = pl.BlockSpec(memory_space=pltpu.VMEM)
    return pl.pallas_call(
        gram_kernel,
        out_shape=(
            jax.ShapeDtypeStruct((8, 7, 8, LANES), F32),
            jax.ShapeDtypeStruct((IB, SLOTS, LANES), BF),
        ),
        in_specs=[pl.BlockSpec(memory_space=pltpu.SMEM), vmem, vmem, vmem],
        out_specs=(vmem, vmem),
        scratch_shapes=[
            pltpu.VMEM((8, 16, IB, LANES), BF),
            pltpu.VMEM((16, 8, ROWS2, LANES), BF),
            pltpu.VMEM((SLOTS * IB, LANES), F32),
            pltpu.VMEM((SLOTS, SLOTS), F32),
            pltpu.VMEM((8, 7, 8, LANES), F32),
            pltpu.VMEM((8, 7, 8, LANES), F32),
            pltpu.VMEM((7, 8, LANES), F32),
            pltpu.VMEM((16, 8, LANES), F32),
            pltpu.VMEM((8, LANES), F32),
            pltpu.VMEM((7, 8, LANES), F32),
            dma((16,)), dma((16,)), dma((8,)), dma((8,)), dma((8,)), dma((8,)),
            dma((8,)), dma((8,)), dma((8,)), dma((8,)),
            dma((8,)), dma((8,)), dma((8,)), dma((16,)), dma((16,)), dma((8,)), dma((8,)), dma((8,)),
        ],
        compiler_params=pltpu.CompilerParams(
            collective_id=0, has_side_effects=True, vmem_limit_bytes=48 * 1024 * 1024),
        name="gram",
    )(energy, lin, cin, slots)


def split3(x):
    high = x.astype(BF)
    rest = x - high.astype(F32)
    mid = rest.astype(BF)
    return high, mid, (rest - mid.astype(F32)).astype(BF)


def recip(x):
    r = pl.reciprocal(x, approx=True)
    return r * (2.0 - x * r)


def sweep(W, n, B):
    sub = lax.broadcasted_iota(jnp.int32, (B, LANES), 0)
    lane = lax.broadcasted_iota(jnp.int32, (B, LANES), 1)
    masks = [sub == i for i in range(B)]
    T = n // LANES

    def chain(k, p):
        t0, l0 = (B * k) // LANES, (B * k) % LANES
        c = [jnp.broadcast_to(p[t0][:, l0 + j:l0 + j + 1], (B, LANES)) for j in range(B)]
        p = list(p)
        for i in range(B):
            inv = recip(c[i][i:i + 1, :])
            ci = c[i]
            for j in range(B):
                if j == i:
                    c[j] = jnp.where(masks[i], inv, -ci * inv)
                else:
                    t = c[j][i:i + 1, :] * inv
                    c[j] = jnp.where(masks[i], t, c[j] - ci * t)
            for v in range(T + 1):
                r = p[v][i:i + 1, :] * inv
                p[v] = jnp.where(masks[i], r, p[v] - ci * r)
        dinv = jnp.zeros((B, LANES), F32)
        for j in range(B):
            dinv = jnp.where(lane == l0 + j, c[j], dinv)
        inside = (lane >= l0) & (lane < l0 + B)
        ident = jnp.where(lane == l0 + sub, 1.0, 0.0)
        x, xs = list(p), list(p)
        x[t0] = jnp.where(inside, ident - dinv, p[t0])
        xs[t0] = jnp.where(inside, -dinv, p[t0])
        return x, xs

    def stack(p, x):
        ph, pm, pl_ = split3(p)
        xh, xm, xl = split3(x)
        join = lambda *parts: jnp.concatenate([q.astype(F32) for q in parts], axis=0).astype(BF)
        return join(ph, ph, pm, ph, pl_, pm), join(xh, xm, xh, xl, xh, xm)

    cat = lambda v: jnp.concatenate(v, axis=1)
    tn = (((0,), (0,)), ((), ()))
    p = [W[0:B, v * LANES:(v + 1) * LANES] for v in range(T + 1)]
    old = None
    for k in range(n // B):
        if old is not None:
            po, xo, xso = old
            ps, xs = stack(cat(po[:T]), cat(xo))
            W[...] = W[...] - lax.dot_general(ps, xs, tn, preferred_element_type=F32)
            W[B * (k - 1):B * k, :] = cat(xso)
        x, xs = chain(k, p)
        old = (p, x, xs)
        if k + 1 < n // B:
            nxt = [W[B * (k + 1):B * (k + 2), v * LANES:(v + 1) * LANES] for v in range(T + 1)]
            t0, l0 = (B * k) // LANES, (B * k) % LANES
            cols = [nxt[t0][:, l0 + i:l0 + i + 1] for i in range(B)]
            for v in range(T + 1):
                terms = [cols[i] * x[v][i:i + 1, :] for i in range(B)]
                while len(terms) > 1:
                    terms = [terms[q] + terms[q + 1] for q in range(0, len(terms), 2)]
                nxt[v] = nxt[v] - terms[0]
            p = nxt
    po, xo, xso = old
    ps, xs = stack(cat(po[:T]), xo[T])
    return W[:, n:] - lax.dot_general(ps, xs, tn, preferred_element_type=F32), xso[T]


def solve_kernel(damp_ref, gt_ref, w_ref, W):
    n, B = SLOTS, 8
    for t in range(48):
        blk, w = t // 16, t % 16
        r0 = (0, 128, 128)[blk] + 8 * w
        c0 = (0, 0, 128)[blk]
        W[r0:r0 + 8, c0:c0 + 128] = gt_ref[t // 6, t % 6]
    W[0:128, 128:256] = W[128:256, 0:128].T
    energy = gt_ref[0, 6]
    e_row = jnp.concatenate([energy[0:1, :], energy[1:2, :]], axis=1)
    sh = e_row - jnp.sum(e_row, axis=1, keepdims=True) * (1.0 / n)
    rows = lax.broadcasted_iota(jnp.int32, (n, n), 0)
    cols = lax.broadcasted_iota(jnp.int32, (n, n), 1)
    eye = rows == cols
    W[:, 0:n] = W[:, 0:n] + jnp.where(eye, damp_ref[0, 0], 0.0)
    W[:, n:] = jnp.broadcast_to(jnp.sum(jnp.where(eye, sh, 0.0), axis=1, keepdims=True), (n, LANES))
    out, last = sweep(W, n, B)
    w_ref[...] = out
    w_ref[n - B:, :] = last


def solve_call(damping, tiles):
    vmem = pl.BlockSpec(memory_space=pltpu.VMEM)
    return pl.pallas_call(
        solve_kernel,
        out_shape=jax.ShapeDtypeStruct((SLOTS, LANES), F32),
        in_specs=[pl.BlockSpec(memory_space=pltpu.SMEM), vmem],
        out_specs=vmem,
        scratch_shapes=[pltpu.VMEM((SLOTS, SLOTS + LANES), F32)],
        name="solve",
    )(damping, tiles)


def update_kernel(w_ref, cen_ref, out_ref, u, send, recv):
    g, d, x_hi, core, z, rb = place()
    a = g * 4 + z
    b = flip(rb, x_hi)
    barrier = pltpu.get_barrier_semaphore()
    for k in range(1, 8):
        pl.semaphore_signal(barrier, inc=1, device_id=column_device(a, (b + k) % 8), device_id_type=MESH)

    scale = -math.sqrt(WIDTH * WIDTH / SLOTS)

    def step(r, carry):
        rows = []
        for v in range(6):
            c = cen_ref[r * 6 + v].astype(F32)
            rows.append(jnp.sum(c * w_ref[...], axis=0, keepdims=True) * scale)
        rows.append(jnp.zeros((2, LANES), F32))
        u[r] = jnp.concatenate(rows, axis=0)
        return carry

    lax.fori_loop(0, 8, step, 0)
    pl.semaphore_wait(barrier, 7)
    sends = []
    for k in range(1, 8):
        rt = (rb + k) % 8
        copy = remote(u.at[rt], out_ref.at[b], send.at[k], recv.at[b], (g, z * 8 + rt))
        copy.start()
        sends.append(copy)
    out_ref[b] = u[rb]
    for k in range(1, 8):
        bs = (b + 8 - k) % 8
        remote(out_ref.at[bs], out_ref.at[bs], send.at[k], recv.at[bs], (g, d)).wait_recv()
    for copy in sends:
        copy.wait_send()


def update_call(weights, cen):
    vmem = pl.BlockSpec(memory_space=pltpu.VMEM)
    return pl.pallas_call(
        update_kernel,
        out_shape=jax.ShapeDtypeStruct((8, 8, LANES), F32),
        in_specs=[vmem, vmem],
        out_specs=vmem,
        scratch_shapes=[pltpu.VMEM((8, 8, LANES), F32), pltpu.SemaphoreType.DMA((8,)), pltpu.SemaphoreType.DMA((8,))],
        compiler_params=pltpu.CompilerParams(
            collective_id=1, has_side_effects=True, vmem_limit_bytes=32 * 1024 * 1024),
        name="update",
    )(weights, cen)


def shards(spin_config, layer_acts, cotangent, patch_embed, energies, slot_sample, damping):
    patches = spin_config.reshape(2, TOKS, -1).astype(F32)
    embedded = jnp.einsum("stk,kd->std", patches, patch_embed.astype(F32))
    layer_in = (layer_acts.astype(F32) + embedded).astype(BF)
    lin = jnp.pad(layer_in.reshape(ROWS2, WIDTH).T, ((0, 0), (0, LANES - ROWS2))).reshape(16, IB, LANES)
    cin = jnp.pad(cotangent.reshape(ROWS2, 8, JB), ((0, 0), (0, 0), (0, LANES - JB))).transpose(1, 0, 2)
    slots = jnp.pad(slot_sample.reshape(2, LANES), ((0, 6), (0, 0)), constant_values=-1)
    tiles, cen = gram_call(energies.reshape(1, 2), lin, cin, slots)
    weights = solve_call(damping.reshape(1, 1), tiles)
    pieces = update_call(weights, cen)
    return pieces[:, :6, :JB].transpose(1, 0, 2).reshape(-1)


def solution(mesh):
    return jax.shard_map(
        shards,
        mesh=mesh,
        in_specs=(
            P(("grp", "dev"), None),
            P(("grp", "dev"), None, None),
            P(("grp", "dev"), None, None),
            P(),
            P(("grp", "dev")),
            P(),
            P(),
        ),
        out_specs=P(("grp", "dev")),
        check_vma=False,
    )
```

```python
import math

import jax
import jax.numpy as jnp
from jax import lax
from jax.experimental import pallas as pl
from jax.experimental.pallas import tpu as pltpu
from jax.sharding import PartitionSpec as P

F32 = jnp.float32
BF = jnp.bfloat16
MESH = pl.DeviceIdType.MESH
SLOTS = 256
WIDTH = 768
TOKS = 36
IB = 48
JB = 96
ROWS2 = 2 * TOKS
LANES = 128


def flip(index, high):
    return index + high * (1 - 2 * (index % 2))


def place():
    g = lax.axis_index("grp")
    d = lax.axis_index("dev")
    x_hi, core = g // 2, g % 2
    z, rb = d // 8, d % 8
    return g, d, x_hi, core, z, rb


def column_device(a, b):
    g, z = a // 4, a % 4
    return (g, z * 8 + flip(b, g // 2))


def remote(src, dst, send_sem, recv_sem, device):
    return pltpu.make_async_remote_copy(
        src_ref=src, dst_ref=dst, send_sem=send_sem, recv_sem=recv_sem,
        device_id=device, device_id_type=MESH,
    )


def rel(r):
    m = r // 2
    return r % 2, m + (m // 2) * (1 - 2 * (m % 2))


def gram_kernel(lin_ref, cin_ref, slot_ref, out_ref, erow_ref, cen_ref,
                lraw, lpk, call, rbuf, esc, gacc, gp, cbuf, rr, s1, cr, s2,
                l1s, l1r, c1s, c1r, c2s, c2r, c3s, c3r, l2s, l2r,
                a_s, a_r, b_s, b_r, x_s, x_r, d_s, d_r, e_s, e_r):
    g, d, x_hi, core, z, rb = place()
    a = g * 4 + z
    b = flip(rb, x_hi)
    q, y = b % 2, b // 2
    partner = (x_hi * 2 + 1 - core, d)

    def cpos(du, dv, other=0):
        c = core + other * (1 - 2 * core)
        return (((x_hi + du) % 2) * 2 + c) * 4 + (z + dv) % 4

    def lpos(du, dv):
        return ((y + dv) % 4) * 2 + (q + du) % 2

    barrier = pltpu.get_barrier_semaphore()
    for k in range(1, 16):
        pl.semaphore_signal(barrier, inc=1, device_id=column_device((a + k) % 16, b), device_id_type=MESH)
    for k in range(1, 8):
        pl.semaphore_signal(barrier, inc=1, device_id=column_device(a, (b + k) % 8), device_id_type=MESH)
    pl.semaphore_wait(barrier, 22)

    sends = []

    def start(copy):
        copy.start()
        sends.append(copy)

    def arrived(ref, sem):
        remote(ref, ref, sem, sem, partner).wait_recv()

    for k in range(1, 8):
        bt = (b + k) % 8
        start(remote(cin_ref.at[bt], call.at[a, b], c1s.at[k], c1r.at[b], column_device(a, bt)))
    for k in range(1, 16):
        at = (a + k) % 16
        start(remote(lin_ref.at[at], lraw.at[a], l1s.at[k], l1r.at[a], column_device(at, b)))
    call[a, b] = cin_ref[b]
    lraw[a] = lin_ref[a]

    def chalf(p, h):
        return call.at[p] if h is None else call.at[p, pl.ds(4 * h, 4)]

    def lhalf(p, h):
        return lpk.at[p] if h is None else lpk.at[p, pl.ds(5 * h, 5 - h)]

    slot_c, slot_l = [0], [0]

    def csend(org, h, to, seen):
        ref = chalf(cpos(*org), h)
        start(remote(ref, ref, c2s.at[slot_c[0]], c2r.at[seen[0] * 4 + seen[1], h or 0], column_device(cpos(*to), b)))
        slot_c[0] += 1

    def lsend(org, h, to, seen):
        ref = lhalf(lpos(*org), h)
        start(remote(ref, ref, l2s.at[slot_l[0]], l2r.at[seen[0] * 4 + seen[1], h or 0], column_device(a, lpos(*to))))
        slot_l[0] += 1

    def over(org, h=None):
        ref = chalf(cpos(*org), h)
        n = org[0] * 4 + org[1]
        start(remote(ref, ref, c3s.at[n, h or 0], c3r.at[n, h or 0], partner))

    def cwait(org, h=None):
        arrived(chalf(cpos(*org), h), c2r.at[org[0] * 4 + org[1], h or 0])

    def owait(org, h=None):
        arrived(chalf(cpos(*org, 1), h), c3r.at[org[0] * 4 + org[1], h or 0])

    def lwait(org, h=None):
        arrived(lhalf(lpos(*org), h), l2r.at[org[0] * 4 + org[1], h or 0])

    HERE, PAIR, UP, DOWN = (0, 0), (1, 0), (0, 1), (0, 3)

    for k in range(1, 8):
        bs = (b + 8 - k) % 8
        arrived(call.at[a, bs], c1r.at[bs])
    csend(HERE, None, PAIR, (1, 0))
    csend(HERE, None, UP, (0, 3))
    csend(HERE, None, DOWN, (0, 1))
    over(HERE)

    for k in range(1, 16):
        asrc = (a + 16 - k) % 16
        arrived(lraw.at[asrc], l1r.at[asrc])
    packed = jnp.concatenate([lraw[s][:, :ROWS2] for s in range(16)], axis=1)
    for t in range(9):
        lpk[b, t] = packed[:, t * LANES:(t + 1) * LANES]
    lsend(HERE, None, PAIR, (1, 0))
    lsend(HERE, None, UP, (0, 3))
    lsend(HERE, None, DOWN, (0, 1))

    cwait(PAIR)
    csend(PAIR, None, UP, (1, 3))
    csend(PAIR, None, DOWN, (1, 1))
    over(PAIR)
    lwait(PAIR)
    lsend(PAIR, None, UP, (1, 3))
    lsend(PAIR, None, DOWN, (1, 1))
    for u in range(2):
        cwait((u, 3))
        csend((u, 3), 0, UP, (u, 2))
        over((u, 3))
        cwait((u, 1))
        csend((u, 1), 1, DOWN, (u, 2))
        over((u, 1))
        lwait((u, 3))
        lsend((u, 3), 0, UP, (u, 2))
        lwait((u, 1))
        lsend((u, 1), 1, DOWN, (u, 2))

    lane = lax.broadcasted_iota(jnp.int32, (IB, LANES), 1)
    first = jnp.where(lane < TOKS, 1.0, 0.0)
    second = jnp.where((lane >= TOKS) & (lane < ROWS2), 1.0, 0.0)
    lane1 = lax.broadcasted_iota(jnp.int32, (1, LANES), 1)
    scale = jnp.where(lane1 < JB, 1.0 / math.sqrt(TOKS), 0.0)

    def rows_of(other, rc, lsteps):
        asrc = cpos(*rel(rc), other)
        off = asrc * ROWS2
        t0 = off // LANES
        o = off % LANES
        t1 = jnp.minimum(t0 + 1, 8)
        shift = (LANES - o) % LANES
        for rl in lsteps:
            bs = lpos(*rel(rl))
            lo = pltpu.roll(lpk[bs, t0].astype(F32), shift, 1)
            hi = pltpu.roll(lpk[bs, t1].astype(F32), shift, 1)
            left = jnp.where(lane < LANES - o, lo, hi)
            left = jnp.concatenate([left * first, left * second], axis=0).astype(BF)
            right = call[asrc, bs]
            prod = lax.dot_general(left[:, :ROWS2], right, (((1,), (0,)), ((), ())), preferred_element_type=F32)
            at = asrc * 8 + flip(bs, asrc // 8)
            rbuf[pl.ds(pl.multiple_of(at * 2 * IB, 2 * IB), 2 * IB), :] = (prod * scale).astype(BF).astype(F32)
            esc[pl.ds(at, 1), :] = right.astype(F32)[0:1, :]

    def rows_loop(other, lo, hi, lsteps):
        def body(rc, carry):
            rows_of(other, rc, lsteps)
            return carry
        lax.fori_loop(lo, hi, body, 0)

    rows_loop(0, 0, 6, range(6))
    for org in (HERE, PAIR, DOWN, UP, (1, 3), (1, 1)):
        owait(org)
    rows_loop(1, 0, 6, range(6))
    for u in range(2):
        for h in range(2):
            cwait((u, 2), h)
            over((u, 2), h)
        for h in range(2):
            lwait((u, 2), h)
    for other in range(2):
        rows_loop(other, 0, 6, range(6, 8))
    rows_loop(0, 6, 8, range(8))
    for u in range(2):
        for h in range(2):
            owait((u, 2), h)
    rows_loop(1, 6, 8, range(8))

    parts = esc[...]
    pos = lax.broadcasted_iota(jnp.int32, (LANES, LANES), 0) * 2
    for half in range(2):
        row = jnp.zeros((1, LANES), F32)
        for k in range(2):
            e = parts[:, JB + 3 * k:JB + 3 * k + 1] + parts[:, JB + 3 * k + 1:JB + 3 * k + 2] + parts[:, JB + 3 * k + 2:JB + 3 * k + 3]
            hit = slot_ref[half:half + 1, :] == pos + k
            row = row + jnp.sum(jnp.where(hit, e, 0.0), axis=0, keepdims=True)
        erow_ref[half:half + 1, :] = row

    gacc[...] = jnp.zeros_like(gacc)
    inv_root = 1.0 / math.sqrt(WIDTH * WIDTH)

    def gram_step(step, carry):
        parts = []
        for u in range(4):
            i = step * 4 + u
            x = rbuf[pl.ds(i, SLOTS, stride=IB), :]
            mean = jnp.sum(x, axis=0, keepdims=True) * (1.0 / SLOTS)
            c = ((x - mean) * inv_root).astype(BF)
            cen_ref[i] = c
            parts.append(c)
        c = jnp.concatenate(parts, axis=1)
        gacc[...] += lax.dot_general(c, c, (((1,), (1,)), ((), ())), preferred_element_type=F32)
        return carry

    lax.fori_loop(0, IB // 4, gram_step, 0)

    for t in range(48):
        blk, w = t // 16, t % 16
        r0 = (0, 128, 128)[blk] + 8 * w
        c0 = (0, 0, 128)[blk]
        gp[t // 24, (t % 24) // 3, t % 3] = gacc[r0:r0 + 8, c0:c0 + 128]

    start(remote(gp.at[1 - core], cbuf, a_s, a_r, partner))
    arrived(cbuf, a_r)
    cbuf[...] = cbuf[...] + gp[core]
    for k in range(1, 8):
        bt = (b + k) % 8
        start(remote(cbuf.at[bt], rr.at[b], b_s.at[k], b_r.at[b], column_device(a, bt)))
    rr[b] = cbuf[b]
    for k in range(1, 8):
        bs = (b + 8 - k) % 8
        arrived(rr.at[bs], b_r.at[bs])
    total = rr[0]
    for k in range(1, 8):
        total = total + rr[k]
    s1[...] = total
    chip = x_hi * 4 + z
    cr[chip] = total
    for k in range(1, 8):
        ct = (chip + k) % 8
        start(remote(s1, cr.at[chip], x_s.at[k], x_r.at[chip], column_device((ct // 4) * 8 + core * 4 + ct % 4, b)))
    for k in range(1, 8):
        cs = (chip + 8 - k) % 8
        arrived(cr.at[cs], x_r.at[cs])
    total = cr[0]
    for k in range(1, 8):
        total = total + cr[k]
    s2[...] = total
    out_ref[core, b] = total
    for k in range(1, 8):
        bt = (b + k) % 8
        start(remote(s2, out_ref.at[core, b], d_s.at[k], d_r.at[b], column_device(a, bt)))
    start(remote(s2, out_ref.at[core, b], e_s.at[0], e_r.at[b], partner))
    for k in range(1, 8):
        bs = (b + 8 - k) % 8
        arrived(out_ref.at[core, bs], d_r.at[bs])
        start(remote(out_ref.at[core, bs], out_ref.at[core, bs], e_s.at[k], e_r.at[bs], partner))
    for k in range(8):
        bs = (b + 8 - k) % 8
        arrived(out_ref.at[1 - core, bs], e_r.at[bs])

    for copy in sends:
        copy.wait_send()


def gram_call(lin, cin, slots):
    dma = pltpu.SemaphoreType.DMA
    vmem = pl.BlockSpec(memory_space=pltpu.VMEM)
    return pl.pallas_call(
        gram_kernel,
        out_shape=(
            jax.ShapeDtypeStruct((2, 8, 3, 8, LANES), F32),
            jax.ShapeDtypeStruct((2, LANES), F32),
            jax.ShapeDtypeStruct((IB, SLOTS, LANES), BF),
        ),
        in_specs=[vmem, vmem, vmem],
        out_specs=(vmem, vmem, vmem),
        scratch_shapes=[
            pltpu.VMEM((16, IB, LANES), BF),
            pltpu.VMEM((8, 9, IB, LANES), BF),
            pltpu.VMEM((16, 8, ROWS2, LANES), BF),
            pltpu.VMEM((SLOTS * IB, LANES), F32),
            pltpu.VMEM((LANES, LANES), F32),
            pltpu.VMEM((SLOTS, SLOTS), F32),
            pltpu.VMEM((2, 8, 3, 8, LANES), F32),
            pltpu.VMEM((8, 3, 8, LANES), F32),
            pltpu.VMEM((8, 3, 8, LANES), F32),
            pltpu.VMEM((3, 8, LANES), F32),
            pltpu.VMEM((8, 3, 8, LANES), F32),
            pltpu.VMEM((3, 8, LANES), F32),
            dma((16,)), dma((16,)), dma((8,)), dma((8,)), dma((9,)), dma((8, 2)),
            dma((8, 2)), dma((8, 2)), dma((9,)), dma((8, 2)),
            dma(()), dma(()), dma((8,)), dma((8,)), dma((8,)), dma((8,)), dma((8,)), dma((8,)), dma((8,)), dma((8,)),
        ],
        compiler_params=pltpu.CompilerParams(
            collective_id=0, has_side_effects=True, vmem_limit_bytes=48 * 1024 * 1024),
        name="gram",
    )(lin, cin, slots)


def split3(x):
    high = x.astype(BF)
    rest = x - high.astype(F32)
    mid = rest.astype(BF)
    return high, mid, (rest - mid.astype(F32)).astype(BF)


def recip(x):
    r = pl.reciprocal(x, approx=True)
    return r * (2.0 - x * r)


def sweep(W, n, B):
    sub = lax.broadcasted_iota(jnp.int32, (B, LANES), 0)
    lane = lax.broadcasted_iota(jnp.int32, (B, LANES), 1)
    masks = [sub == i for i in range(B)]
    T = n // LANES

    def chain(k, p):
        t0, l0 = (B * k) // LANES, (B * k) % LANES
        c = [jnp.broadcast_to(p[t0][:, l0 + j:l0 + j + 1], (B, LANES)) for j in range(B)]
        p = list(p)
        for i in range(B):
            inv = recip(c[i][i:i + 1, :])
            ci = c[i]
            for j in range(B):
                if j == i:
                    c[j] = jnp.where(masks[i], inv, -ci * inv)
                else:
                    t = c[j][i:i + 1, :] * inv
                    c[j] = jnp.where(masks[i], t, c[j] - ci * t)
            for v in range(T + 1):
                r = p[v][i:i + 1, :] * inv
                p[v] = jnp.where(masks[i], r, p[v] - ci * r)
        dinv = jnp.zeros((B, LANES), F32)
        for j in range(B):
            dinv = jnp.where(lane == l0 + j, c[j], dinv)
        inside = (lane >= l0) & (lane < l0 + B)
        ident = jnp.where(lane == l0 + sub, 1.0, 0.0)
        x, xs = list(p), list(p)
        x[t0] = jnp.where(inside, ident - dinv, p[t0])
        xs[t0] = jnp.where(inside, -dinv, p[t0])
        return x, xs

    def stack(p, x):
        ph, pm, pl_ = split3(p)
        xh, xm, xl = split3(x)
        join = lambda *parts: jnp.concatenate([q.astype(F32) for q in parts], axis=0).astype(BF)
        return join(ph, ph, pm, ph, pl_, pm), join(xh, xm, xh, xl, xh, xm)

    cat = lambda v: jnp.concatenate(v, axis=1)
    tn = (((0,), (0,)), ((), ()))
    p = [W[0:B, v * LANES:(v + 1) * LANES] for v in range(T + 1)]
    old = None
    for k in range(n // B):
        if old is not None:
            po, xo, xso = old
            ps, xs = stack(cat(po[:T]), cat(xo))
            W[...] = W[...] - lax.dot_general(ps, xs, tn, preferred_element_type=F32)
            W[B * (k - 1):B * k, :] = cat(xso)
        x, xs = chain(k, p)
        old = (p, x, xs)
        if k + 1 < n // B:
            nxt = [W[B * (k + 1):B * (k + 2), v * LANES:(v + 1) * LANES] for v in range(T + 1)]
            t0, l0 = (B * k) // LANES, (B * k) % LANES
            cols = [nxt[t0][:, l0 + i:l0 + i + 1] for i in range(B)]
            for v in range(T + 1):
                terms = [cols[i] * x[v][i:i + 1, :] for i in range(B)]
                while len(terms) > 1:
                    terms = [terms[q] + terms[q + 1] for q in range(0, len(terms), 2)]
                nxt[v] = nxt[v] - terms[0]
            p = nxt
    po, xo, xso = old
    ps, xs = stack(cat(po[:T]), xo[T])
    return W[:, n:] - lax.dot_general(ps, xs, tn, preferred_element_type=F32), xso[T]


def solve_kernel(damp_ref, gt_ref, erow_ref, w_ref, W):
    n, B = SLOTS, 8
    for t in range(48):
        blk, w = t // 16, t % 16
        r0 = (0, 128, 128)[blk] + 8 * w
        c0 = (0, 0, 128)[blk]
        W[r0:r0 + 8, c0:c0 + 128] = gt_ref[t // 24, (t % 24) // 3, t % 3]
    W[0:128, 128:256] = W[128:256, 0:128].T
    e_row = jnp.concatenate([erow_ref[0:1, :], erow_ref[1:2, :]], axis=1)
    sh = e_row - jnp.sum(e_row, axis=1, keepdims=True) * (1.0 / n)
    rows = lax.broadcasted_iota(jnp.int32, (n, n), 0)
    cols = lax.broadcasted_iota(jnp.int32, (n, n), 1)
    eye = rows == cols
    W[:, 0:n] = W[:, 0:n] + jnp.where(eye, damp_ref[0, 0], 0.0)
    W[:, n:] = jnp.broadcast_to(jnp.sum(jnp.where(eye, sh, 0.0), axis=1, keepdims=True), (n, LANES))
    out, last = sweep(W, n, B)
    w_ref[...] = out
    w_ref[n - B:, :] = last


def solve_call(damping, tiles, erow):
    vmem = pl.BlockSpec(memory_space=pltpu.VMEM)
    return pl.pallas_call(
        solve_kernel,
        out_shape=jax.ShapeDtypeStruct((SLOTS, LANES), F32),
        in_specs=[pl.BlockSpec(memory_space=pltpu.SMEM), vmem, vmem],
        out_specs=vmem,
        scratch_shapes=[pltpu.VMEM((SLOTS, SLOTS + LANES), F32)],
        name="solve",
    )(damping, tiles, erow)


def update_kernel(w_ref, cen_ref, out_ref, u, send, recv):
    g, d, x_hi, core, z, rb = place()
    a = g * 4 + z
    b = flip(rb, x_hi)
    barrier = pltpu.get_barrier_semaphore()
    for k in range(1, 8):
        pl.semaphore_signal(barrier, inc=1, device_id=column_device(a, (b + k) % 8), device_id_type=MESH)

    scale = -math.sqrt(WIDTH * WIDTH / SLOTS)

    def step(r, carry):
        rows = []
        for v in range(6):
            c = cen_ref[r * 6 + v].astype(F32)
            rows.append(jnp.sum(c * w_ref[...], axis=0, keepdims=True) * scale)
        rows.append(jnp.zeros((2, LANES), F32))
        u[r] = jnp.concatenate(rows, axis=0)
        return carry

    lax.fori_loop(0, 8, step, 0)
    pl.semaphore_wait(barrier, 7)
    sends = []
    for k in range(1, 8):
        rt = (rb + k) % 8
        copy = remote(u.at[rt], out_ref.at[b], send.at[k], recv.at[b], (g, z * 8 + rt))
        copy.start()
        sends.append(copy)
    out_ref[b] = u[rb]
    for k in range(1, 8):
        bs = (b + 8 - k) % 8
        remote(out_ref.at[bs], out_ref.at[bs], send.at[k], recv.at[bs], (g, d)).wait_recv()
    for copy in sends:
        copy.wait_send()


def update_call(weights, cen):
    vmem = pl.BlockSpec(memory_space=pltpu.VMEM)
    return pl.pallas_call(
        update_kernel,
        out_shape=jax.ShapeDtypeStruct((8, 8, LANES), F32),
        in_specs=[vmem, vmem],
        out_specs=vmem,
        scratch_shapes=[pltpu.VMEM((8, 8, LANES), F32), pltpu.SemaphoreType.DMA((8,)), pltpu.SemaphoreType.DMA((8,))],
        compiler_params=pltpu.CompilerParams(
            collective_id=1, has_side_effects=True, vmem_limit_bytes=32 * 1024 * 1024),
        name="update",
    )(weights, cen)


def shards(spin_config, layer_acts, cotangent, patch_embed, energies, slot_sample, damping):
    patches = spin_config.reshape(2, TOKS, -1).astype(F32)
    embedded = jnp.einsum("stk,kd->std", patches, patch_embed.astype(F32))
    layer_in = (layer_acts.astype(F32) + embedded).astype(BF)
    lin = jnp.pad(layer_in.reshape(ROWS2, WIDTH).T, ((0, 0), (0, LANES - ROWS2))).reshape(16, IB, LANES)
    cin = jnp.pad(cotangent.reshape(ROWS2, 8, JB), ((0, 0), (0, 0), (0, LANES - JB))).transpose(1, 0, 2)
    high = lax.reduce_precision(energies, 8, 7)
    mid = lax.reduce_precision(energies - high, 8, 7)
    parts = jnp.stack([high, mid, energies - high - mid], axis=1).reshape(1, 1, 6).astype(BF)
    parts = jnp.pad(parts, ((0, 0), (0, ROWS2 - 1), (JB, LANES - JB - 6)))
    cin = cin + parts
    tiles, erow, cen = gram_call(lin, cin, slot_sample.reshape(2, LANES))
    weights = solve_call(damping.reshape(1, 1), tiles, erow)
    pieces = update_call(weights, cen)
    return pieces[:, :6, :JB].transpose(1, 0, 2).reshape(-1)


def solution(mesh):
    return jax.shard_map(
        shards,
        mesh=mesh,
        in_specs=(
            P(("grp", "dev"), None),
            P(("grp", "dev"), None, None),
            P(("grp", "dev"), None, None),
            P(),
            P(("grp", "dev")),
            P(),
            P(),
        ),
        out_specs=P(("grp", "dev")),
        check_vma=False,
    )
```

```python
import math

import jax
import jax.numpy as jnp
from jax import lax
from jax.experimental import pallas as pl
from jax.experimental.pallas import tpu as pltpu
from jax.sharding import PartitionSpec as P

F32 = jnp.float32
BF = jnp.bfloat16
MESH = pl.DeviceIdType.MESH
SLOTS = 256
WIDTH = 768
SITES = 144
PATCH = 4
TOKS = 36
IB = 48
JB = 96
ROWS2 = 2 * TOKS
LANES = 128


def flip(index, high):
    return index + high * (1 - 2 * (index % 2))


def place():
    g = lax.axis_index("grp")
    d = lax.axis_index("dev")
    x_hi, core = g // 2, g % 2
    z, rb = d // 8, d % 8
    return g, d, x_hi, core, z, rb


def column_device(a, b):
    g, z = a // 4, a % 4
    return (g, z * 8 + flip(b, g // 2))


def remote(src, dst, send_sem, recv_sem, device):
    return pltpu.make_async_remote_copy(
        src_ref=src, dst_ref=dst, send_sem=send_sem, recv_sem=recv_sem,
        device_id=device, device_id_type=MESH,
    )


def rel(r):
    m = r // 2
    return r % 2, m + (m // 2) * (1 - 2 * (m % 2))


def split3(x):
    high = x.astype(BF)
    rest = x - high.astype(F32)
    mid = rest.astype(BF)
    return high, mid, (rest - mid.astype(F32)).astype(BF)


def recip(x):
    r = pl.reciprocal(x, approx=True)
    return r * (2.0 - x * r)


def sweep(W, n, B):
    sub = lax.broadcasted_iota(jnp.int32, (B, LANES), 0)
    lane = lax.broadcasted_iota(jnp.int32, (B, LANES), 1)
    masks = [sub == i for i in range(B)]
    T = n // LANES

    def chain(k, p):
        t0, l0 = (B * k) // LANES, (B * k) % LANES
        c = [jnp.broadcast_to(p[t0][:, l0 + j:l0 + j + 1], (B, LANES)) for j in range(B)]
        p = list(p)
        for i in range(B):
            inv = recip(c[i][i:i + 1, :])
            ci = c[i]
            for j in range(B):
                if j == i:
                    c[j] = jnp.where(masks[i], inv, -ci * inv)
                else:
                    t = c[j][i:i + 1, :] * inv
                    c[j] = jnp.where(masks[i], t, c[j] - ci * t)
            for v in range(T + 1):
                r = p[v][i:i + 1, :] * inv
                p[v] = jnp.where(masks[i], r, p[v] - ci * r)
        dinv = jnp.zeros((B, LANES), F32)
        for j in range(B):
            dinv = jnp.where(lane == l0 + j, c[j], dinv)
        inside = (lane >= l0) & (lane < l0 + B)
        ident = jnp.where(lane == l0 + sub, 1.0, 0.0)
        x, xs = list(p), list(p)
        x[t0] = jnp.where(inside, ident - dinv, p[t0])
        xs[t0] = jnp.where(inside, -dinv, p[t0])
        return x, xs

    def stack(p, x):
        ph, pm, pl_ = split3(p)
        xh, xm, xl = split3(x)
        join = lambda *parts: jnp.concatenate([q.astype(F32) for q in parts], axis=0).astype(BF)
        return join(ph, ph, pm, ph, pl_, pm), join(xh, xm, xh, xl, xh, xm)

    cat = lambda v: jnp.concatenate(v, axis=1)
    tn = (((0,), (0,)), ((), ()))
    p = [W[0:B, v * LANES:(v + 1) * LANES] for v in range(T + 1)]
    old = None
    for k in range(n // B):
        if old is not None:
            po, xo, xso = old
            ps, xs = stack(cat(po[:T]), cat(xo))
            W[...] = W[...] - lax.dot_general(ps, xs, tn, preferred_element_type=F32)
            W[B * (k - 1):B * k, :] = cat(xso)
        x, xs = chain(k, p)
        old = (p, x, xs)
        if k + 1 < n // B:
            nxt = [W[B * (k + 1):B * (k + 2), v * LANES:(v + 1) * LANES] for v in range(T + 1)]
            t0, l0 = (B * k) // LANES, (B * k) % LANES
            cols = [nxt[t0][:, l0 + i:l0 + i + 1] for i in range(B)]
            for v in range(T + 1):
                terms = [cols[i] * x[v][i:i + 1, :] for i in range(B)]
                while len(terms) > 1:
                    terms = [terms[q] + terms[q + 1] for q in range(0, len(terms), 2)]
                nxt[v] = nxt[v] - terms[0]
            p = nxt
    po, xo, xso = old
    ps, xs = stack(cat(po[:T]), xo[T])
    return W[:, n:] - lax.dot_general(ps, xs, tn, preferred_element_type=F32), xso[T]


def prepare(spin, acts, cot, embed, energy_ref, stage, cstage, lin, cin):
    sub = lax.broadcasted_iota(jnp.int32, (40, SITES), 0)
    site = lax.broadcasted_iota(jnp.int32, (40, SITES), 1)
    spins = spin[...].astype(F32)
    patches = jnp.concatenate(
        [jnp.where(site // PATCH == sub, spins[s:s + 1, :], 0.0) for s in range(2)], axis=0).astype(BF)
    turn = lax.broadcasted_iota(jnp.int32, (SITES, WIDTH), 0) % PATCH
    table = embed[...].astype(F32)
    spread = jnp.zeros((SITES, WIDTH), F32)
    for k in range(PATCH):
        spread = jnp.where(turn == k, table[k:k + 1, :], spread)
    added = jnp.dot(patches, spread.astype(BF), preferred_element_type=F32)
    for s in range(2):
        stage[TOKS * s:TOKS * (s + 1), :] = (acts[s].astype(F32) + added[40 * s:40 * s + TOKS, :]).astype(BF).astype(F32)
    stage[ROWS2:, :] = jnp.zeros((LANES - ROWS2, WIDTH), F32)
    for v in range(WIDTH // LANES):
        lin[v * LANES:(v + 1) * LANES, :] = stage[:, v * LANES:(v + 1) * LANES].T.astype(BF)
    lane = lax.broadcasted_iota(jnp.int32, (TOKS, LANES), 1)
    row = lax.broadcasted_iota(jnp.int32, (TOKS, LANES), 0)
    high, mid, low = (t.astype(F32) for t in split3(
        jnp.where(lane < JB + 3, jnp.full((TOKS, LANES), energy_ref[0], F32), jnp.full((TOKS, LANES), energy_ref[1], F32))))
    third = lane % 3
    parts = jnp.where(third == 0, high, jnp.where(third == 1, mid, low))
    parts = jnp.where((row == 0) & (lane < JB + 6), parts, 0.0)
    for s in range(2):
        x = cot[s].astype(F32)
        for b in range(8):
            t, o = (JB * b) // LANES, (JB * b) % LANES
            piece = x[:, t * LANES:(t + 1) * LANES]
            if o:
                piece = pltpu.roll(piece, LANES - o, 1)
                if LANES - o < JB:
                    piece = jnp.where(lane < LANES - o, piece, pltpu.roll(x[:, (t + 1) * LANES:(t + 2) * LANES], LANES - o, 1))
            cstage[b, TOKS * s:TOKS * (s + 1), :] = jnp.where(lane < JB, piece, parts if s == 0 else 0.0)
    cin[...] = cstage[...].astype(BF)


def main_kernel(energy_ref, damp_ref, spin_hbm, acts_hbm, cot_hbm, embed_hbm, slot_hbm, out_ref,
                spin_v, acts_v, cot_v, embed_v, slot_ref, in_sem, stage, cstage, lin_ref, cin_ref,
                gt, erow_ref, cen_ref, W, wv, upd, ur, f_s, f_r,
                lraw, lpk, call, rbuf, esc, gacc, gp, cbuf, rr, s1, cr, s2,
                l1s, l1r, c1s, c1r, c2s, c2r, c3s, c3r, l2s, l2r,
                a_s, a_r, b_s, b_r, x_s, x_r, d_s, d_r, e_s, e_r):
    g, d, x_hi, core, z, rb = place()
    a = g * 4 + z
    b = flip(rb, x_hi)
    q, y = b % 2, b // 2
    partner = (x_hi * 2 + 1 - core, d)

    def cpos(du, dv, other=0):
        c = core + other * (1 - 2 * core)
        return (((x_hi + du) % 2) * 2 + c) * 4 + (z + dv) % 4

    def lpos(du, dv):
        return ((y + dv) % 4) * 2 + (q + du) % 2

    barrier = pltpu.get_barrier_semaphore()
    for k in range(1, 16):
        pl.semaphore_signal(barrier, inc=1, device_id=column_device((a + k) % 16, b), device_id_type=MESH)
    for k in range(1, 8):
        pl.semaphore_signal(barrier, inc=1, device_id=column_device(a, (b + k) % 8), device_id_type=MESH)
    loads = [pltpu.make_async_copy(src, dst, in_sem.at[n]) for n, (src, dst) in enumerate(
        ((spin_hbm, spin_v), (acts_hbm, acts_v), (cot_hbm, cot_v), (embed_hbm, embed_v), (slot_hbm, slot_ref)))]
    for copy in loads:
        copy.start()
    for copy in loads:
        copy.wait()
    prepare(spin_v, acts_v, cot_v, embed_v, energy_ref, stage, cstage, lin_ref, cin_ref)
    pl.semaphore_wait(barrier, 22)

    sends = []

    def start(copy):
        copy.start()
        sends.append(copy)

    def arrived(ref, sem):
        remote(ref, ref, sem, sem, partner).wait_recv()

    for k in range(1, 8):
        bt = (b + k) % 8
        start(remote(cin_ref.at[bt], call.at[a, b], c1s.at[k], c1r.at[b], column_device(a, bt)))
    for k in range(1, 16):
        at = (a + k) % 16
        start(remote(lin_ref.at[pl.ds(pl.multiple_of(at * IB, IB), IB)], lraw.at[a], l1s.at[k], l1r.at[a], column_device(at, b)))
    call[a, b] = cin_ref[b]
    lraw[a] = lin_ref[pl.ds(pl.multiple_of(a * IB, IB), IB), :]

    def chalf(p, h):
        return call.at[p] if h is None else call.at[p, pl.ds(4 * h, 4)]

    def lhalf(p, h):
        return lpk.at[p] if h is None else lpk.at[p, pl.ds(5 * h, 5 - h)]

    slot_c, slot_l = [0], [0]

    def csend(org, h, to, seen):
        ref = chalf(cpos(*org), h)
        start(remote(ref, ref, c2s.at[slot_c[0]], c2r.at[seen[0] * 4 + seen[1], h or 0], column_device(cpos(*to), b)))
        slot_c[0] += 1

    def lsend(org, h, to, seen):
        ref = lhalf(lpos(*org), h)
        start(remote(ref, ref, l2s.at[slot_l[0]], l2r.at[seen[0] * 4 + seen[1], h or 0], column_device(a, lpos(*to))))
        slot_l[0] += 1

    def over(org, h=None):
        ref = chalf(cpos(*org), h)
        n = org[0] * 4 + org[1]
        start(remote(ref, ref, c3s.at[n, h or 0], c3r.at[n, h or 0], partner))

    def cwait(org, h=None):
        arrived(chalf(cpos(*org), h), c2r.at[org[0] * 4 + org[1], h or 0])

    def owait(org, h=None):
        arrived(chalf(cpos(*org, 1), h), c3r.at[org[0] * 4 + org[1], h or 0])

    def lwait(org, h=None):
        arrived(lhalf(lpos(*org), h), l2r.at[org[0] * 4 + org[1], h or 0])

    HERE, PAIR, UP, DOWN = (0, 0), (1, 0), (0, 1), (0, 3)

    for k in range(1, 8):
        bs = (b + 8 - k) % 8
        arrived(call.at[a, bs], c1r.at[bs])
    csend(HERE, None, PAIR, (1, 0))
    csend(HERE, None, UP, (0, 3))
    csend(HERE, None, DOWN, (0, 1))
    over(HERE)

    for k in range(1, 16):
        asrc = (a + 16 - k) % 16
        arrived(lraw.at[asrc], l1r.at[asrc])
    packed = jnp.concatenate([lraw[s][:, :ROWS2] for s in range(16)], axis=1)
    for t in range(9):
        lpk[b, t] = packed[:, t * LANES:(t + 1) * LANES]
    lsend(HERE, None, PAIR, (1, 0))
    lsend(HERE, None, UP, (0, 3))
    lsend(HERE, None, DOWN, (0, 1))

    cwait(PAIR)
    csend(PAIR, None, UP, (1, 3))
    csend(PAIR, None, DOWN, (1, 1))
    over(PAIR)
    lwait(PAIR)
    lsend(PAIR, None, UP, (1, 3))
    lsend(PAIR, None, DOWN, (1, 1))
    for u in range(2):
        cwait((u, 3))
        csend((u, 3), 0, UP, (u, 2))
        over((u, 3))
        cwait((u, 1))
        csend((u, 1), 1, DOWN, (u, 2))
        over((u, 1))
        lwait((u, 3))
        lsend((u, 3), 0, UP, (u, 2))
        lwait((u, 1))
        lsend((u, 1), 1, DOWN, (u, 2))

    lane = lax.broadcasted_iota(jnp.int32, (IB, LANES), 1)
    first = jnp.where(lane < TOKS, 1.0, 0.0)
    second = jnp.where((lane >= TOKS) & (lane < ROWS2), 1.0, 0.0)
    lane1 = lax.broadcasted_iota(jnp.int32, (1, LANES), 1)
    scale = jnp.where(lane1 < JB, 1.0 / math.sqrt(TOKS), 0.0)

    def rows_of(other, rc, lsteps):
        asrc = cpos(*rel(rc), other)
        off = asrc * ROWS2
        t0 = off // LANES
        o = off % LANES
        t1 = jnp.minimum(t0 + 1, 8)
        shift = (LANES - o) % LANES
        for rl in lsteps:
            bs = lpos(*rel(rl))
            lo = pltpu.roll(lpk[bs, t0].astype(F32), shift, 1)
            hi = pltpu.roll(lpk[bs, t1].astype(F32), shift, 1)
            left = jnp.where(lane < LANES - o, lo, hi)
            left = jnp.concatenate([left * first, left * second], axis=0).astype(BF)
            right = call[asrc, bs]
            prod = lax.dot_general(left[:, :ROWS2], right, (((1,), (0,)), ((), ())), preferred_element_type=F32)
            at = asrc * 8 + flip(bs, asrc // 8)
            rbuf[pl.ds(pl.multiple_of(at * 2 * IB, 2 * IB), 2 * IB), :] = (prod * scale).astype(BF).astype(F32)
            esc[pl.ds(at, 1), :] = right.astype(F32)[0:1, :]

    def rows_loop(other, lo, hi, lsteps):
        def body(rc, carry):
            rows_of(other, rc, lsteps)
            return carry
        lax.fori_loop(lo, hi, body, 0)

    rows_loop(0, 0, 6, range(6))
    for org in (HERE, PAIR, DOWN, UP, (1, 3), (1, 1)):
        owait(org)
    rows_loop(1, 0, 6, range(6))
    for u in range(2):
        for h in range(2):
            cwait((u, 2), h)
            over((u, 2), h)
        for h in range(2):
            lwait((u, 2), h)
    for other in range(2):
        rows_loop(other, 0, 6, range(6, 8))
    rows_loop(0, 6, 8, range(8))
    for u in range(2):
        for h in range(2):
            owait((u, 2), h)
    rows_loop(1, 6, 8, range(8))

    parts = esc[...]
    pos = lax.broadcasted_iota(jnp.int32, (LANES, LANES), 0) * 2
    for half in range(2):
        row = jnp.zeros((1, LANES), F32)
        for k in range(2):
            e = parts[:, JB + 3 * k:JB + 3 * k + 1] + parts[:, JB + 3 * k + 1:JB + 3 * k + 2] + parts[:, JB + 3 * k + 2:JB + 3 * k + 3]
            hit = slot_ref[half:half + 1, :] == pos + k
            row = row + jnp.sum(jnp.where(hit, e, 0.0), axis=0, keepdims=True)
        erow_ref[half:half + 1, :] = row

    gacc[...] = jnp.zeros_like(gacc)
    inv_root = 1.0 / math.sqrt(WIDTH * WIDTH)

    def gram_step(m, carry):
        xs = [rbuf[pl.ds(pl.multiple_of(s * IB + m * 8, 8), 8), :] for s in range(SLOTS)]
        sums = xs[:8]
        for s in range(8, SLOTS):
            sums[s % 8] = sums[s % 8] + xs[s]
        while len(sums) > 1:
            sums = [sums[n] + sums[n + 1] for n in range(0, len(sums), 2)]
        mean = sums[0] * (1.0 / SLOTS)
        c = jnp.concatenate([((x - mean) * inv_root)[None] for x in xs], axis=0)
        c = jnp.transpose(c, (1, 0, 2)).astype(BF)
        cen_ref[pl.ds(pl.multiple_of(m * 8, 8), 8)] = c
        c = jnp.concatenate([c[n] for n in range(8)], axis=1)
        gacc[...] += lax.dot_general(c, c, (((1,), (1,)), ((), ())), preferred_element_type=F32)
        return carry

    lax.fori_loop(0, IB // 8, gram_step, 0)

    for t in range(48):
        blk, w = t // 16, t % 16
        r0 = (0, 128, 128)[blk] + 8 * w
        c0 = (0, 0, 128)[blk]
        gp[t // 24, (t % 24) // 3, t % 3] = gacc[r0:r0 + 8, c0:c0 + 128]

    start(remote(gp.at[1 - core], cbuf, a_s, a_r, partner))
    arrived(cbuf, a_r)
    cbuf[...] = cbuf[...] + gp[core]
    for k in range(1, 8):
        bt = (b + k) % 8
        start(remote(cbuf.at[bt], rr.at[b], b_s.at[k], b_r.at[b], column_device(a, bt)))
    rr[b] = cbuf[b]
    for k in range(1, 8):
        bs = (b + 8 - k) % 8
        arrived(rr.at[bs], b_r.at[bs])
    total = rr[0]
    for k in range(1, 8):
        total = total + rr[k]
    s1[...] = total
    chip = x_hi * 4 + z
    cr[chip] = total
    for k in range(1, 8):
        ct = (chip + k) % 8
        start(remote(s1, cr.at[chip], x_s.at[k], x_r.at[chip], column_device((ct // 4) * 8 + core * 4 + ct % 4, b)))
    for k in range(1, 8):
        cs = (chip + 8 - k) % 8
        arrived(cr.at[cs], x_r.at[cs])
    total = cr[0]
    for k in range(1, 8):
        total = total + cr[k]
    s2[...] = total
    gt[core, b] = total
    for k in range(1, 8):
        bt = (b + k) % 8
        start(remote(s2, gt.at[core, b], d_s.at[k], d_r.at[b], column_device(a, bt)))
    start(remote(s2, gt.at[core, b], e_s.at[0], e_r.at[b], partner))
    for k in range(1, 8):
        bs = (b + 8 - k) % 8
        arrived(gt.at[core, bs], d_r.at[bs])
        start(remote(gt.at[core, bs], gt.at[core, bs], e_s.at[k], e_r.at[bs], partner))
    for k in range(8):
        bs = (b + 8 - k) % 8
        arrived(gt.at[1 - core, bs], e_r.at[bs])

    for t in range(48):
        blk, w = t // 16, t % 16
        r0 = (0, 128, 128)[blk] + 8 * w
        c0 = (0, 0, 128)[blk]
        W[r0:r0 + 8, c0:c0 + 128] = gt[t // 24, (t % 24) // 3, t % 3]
    W[0:128, 128:256] = W[128:256, 0:128].T
    e_row = jnp.concatenate([erow_ref[0:1, :], erow_ref[1:2, :]], axis=1)
    sh = e_row - jnp.sum(e_row, axis=1, keepdims=True) * (1.0 / SLOTS)
    rows = lax.broadcasted_iota(jnp.int32, (SLOTS, SLOTS), 0)
    cols = lax.broadcasted_iota(jnp.int32, (SLOTS, SLOTS), 1)
    eye = rows == cols
    W[:, 0:SLOTS] = W[:, 0:SLOTS] + jnp.where(eye, damp_ref[0], 0.0)
    W[:, SLOTS:] = jnp.broadcast_to(jnp.sum(jnp.where(eye, sh, 0.0), axis=1, keepdims=True), (SLOTS, LANES))
    weights, last = sweep(W, SLOTS, 8)
    wv[...] = weights
    wv[SLOTS - 8:, :] = last

    step_scale = -math.sqrt(WIDTH * WIDTH / SLOTS)

    def update_step(r, carry):
        done = []
        for v in range(6):
            c = cen_ref[r * 6 + v].astype(F32)
            done.append(jnp.sum(c * wv[...], axis=0, keepdims=True) * step_scale)
        done.append(jnp.zeros((2, LANES), F32))
        upd[r] = jnp.concatenate(done, axis=0)
        return carry

    lax.fori_loop(0, 8, update_step, 0)
    for k in range(1, 8):
        bt = (b + k) % 8
        start(remote(upd.at[flip(bt, x_hi)], ur.at[b], f_s.at[k], f_r.at[b], column_device(a, bt)))
    ur[b] = upd[rb]
    for copy in sends[:-7]:
        copy.wait_send()
    for k in range(1, 8):
        bs = (b + 8 - k) % 8
        arrived(ur.at[bs], f_r.at[bs])
    whole = jnp.concatenate([ur[n][:, :JB] for n in range(8)], axis=1)
    for i in range(6):
        for v in range(6):
            out_ref[6 * i + v:6 * i + v + 1, :] = whole[i:i + 1, v * LANES:(v + 1) * LANES]
    for copy in sends[-7:]:
        copy.wait_send()


def main_call(energies, damping, spin, acts, cot, embed, slots):
    dma = pltpu.SemaphoreType.DMA
    smem = pl.BlockSpec(memory_space=pltpu.SMEM)
    hbm = pl.BlockSpec(memory_space=pl.ANY)
    return pl.pallas_call(
        main_kernel,
        out_shape=jax.ShapeDtypeStruct((36, LANES), F32),
        in_specs=[smem, smem, hbm, hbm, hbm, hbm, hbm],
        out_specs=pl.BlockSpec(memory_space=pltpu.VMEM),
        scratch_shapes=[
            pltpu.VMEM(spin.shape, jnp.int32),
            pltpu.VMEM(acts.shape, BF),
            pltpu.VMEM(cot.shape, BF),
            pltpu.VMEM(embed.shape, BF),
            pltpu.VMEM(slots.shape, jnp.int32),
            dma((5,)),
            pltpu.VMEM((LANES, WIDTH), F32),
            pltpu.VMEM((8, ROWS2, LANES), F32),
            pltpu.VMEM((WIDTH, LANES), BF),
            pltpu.VMEM((8, ROWS2, LANES), BF),
            pltpu.VMEM((2, 8, 3, 8, LANES), F32),
            pltpu.VMEM((2, LANES), F32),
            pltpu.VMEM((IB, SLOTS, LANES), BF),
            pltpu.VMEM((SLOTS, SLOTS + LANES), F32),
            pltpu.VMEM((SLOTS, LANES), F32),
            pltpu.VMEM((8, 8, LANES), F32),
            pltpu.VMEM((8, 8, LANES), F32),
            dma((8,)), dma((8,)),
            pltpu.VMEM((16, IB, LANES), BF),
            pltpu.VMEM((8, 9, IB, LANES), BF),
            pltpu.VMEM((16, 8, ROWS2, LANES), BF),
            pltpu.VMEM((SLOTS * IB, LANES), F32),
            pltpu.VMEM((LANES, LANES), F32),
            pltpu.VMEM((SLOTS, SLOTS), F32),
            pltpu.VMEM((2, 8, 3, 8, LANES), F32),
            pltpu.VMEM((8, 3, 8, LANES), F32),
            pltpu.VMEM((8, 3, 8, LANES), F32),
            pltpu.VMEM((3, 8, LANES), F32),
            pltpu.VMEM((8, 3, 8, LANES), F32),
            pltpu.VMEM((3, 8, LANES), F32),
            dma((16,)), dma((16,)), dma((8,)), dma((8,)), dma((9,)), dma((8, 2)),
            dma((8, 2)), dma((8, 2)), dma((9,)), dma((8, 2)),
            dma(()), dma(()), dma((8,)), dma((8,)), dma((8,)), dma((8,)), dma((8,)), dma((8,)), dma((8,)), dma((8,)),
        ],
        compiler_params=pltpu.CompilerParams(
            collective_id=0, has_side_effects=True, vmem_limit_bytes=48 * 1024 * 1024),
        name="main",
    )(energies, damping, spin, acts, cot, embed, slots)


def shards(spin_config, layer_acts, cotangent, patch_embed, energies, slot_sample, damping):
    out = main_call(energies, damping.reshape(1), spin_config, layer_acts, cotangent, patch_embed,
                    slot_sample.reshape(2, LANES))
    return out.reshape(-1)


def solution(mesh):
    return jax.shard_map(
        shards,
        mesh=mesh,
        in_specs=(
            P(("grp", "dev"), None),
            P(("grp", "dev"), None, None),
            P(("grp", "dev"), None, None),
            P(),
            P(("grp", "dev")),
            P(),
            P(),
        ),
        out_specs=P(("grp", "dev")),
        check_vma=False,
    )
```

```python
import math

import jax
import jax.numpy as jnp
from jax import lax
from jax.experimental import pallas as pl
from jax.experimental.pallas import tpu as pltpu
from jax.sharding import PartitionSpec as P

F32 = jnp.float32
BF = jnp.bfloat16
MESH = pl.DeviceIdType.MESH
SLOTS = 256
WIDTH = 768
SITES = 144
PATCH = 4
TOKS = 36
IB = 48
JB = 96
ROWS2 = 2 * TOKS
LANES = 128


def flip(index, high):
    return index + high * (1 - 2 * (index % 2))


def place():
    g = lax.axis_index("grp")
    d = lax.axis_index("dev")
    x_hi, core = g // 2, g % 2
    z, rb = d // 8, d % 8
    return g, d, x_hi, core, z, rb


def column_device(a, b):
    g, z = a // 4, a % 4
    return (g, z * 8 + flip(b, g // 2))


def remote(src, dst, send_sem, recv_sem, device):
    return pltpu.make_async_remote_copy(
        src_ref=src, dst_ref=dst, send_sem=send_sem, recv_sem=recv_sem,
        device_id=device, device_id_type=MESH,
    )


def rel(r):
    m = r // 2
    return r % 2, m + (m // 2) * (1 - 2 * (m % 2))


def split3(x):
    high = x.astype(BF)
    rest = x - high.astype(F32)
    mid = rest.astype(BF)
    return high, mid, (rest - mid.astype(F32)).astype(BF)


def recip(x):
    r = pl.reciprocal(x, approx=True)
    return r * (2.0 - x * r)


def sweep(W, n, B):
    sub = lax.broadcasted_iota(jnp.int32, (B, LANES), 0)
    lane = lax.broadcasted_iota(jnp.int32, (B, LANES), 1)
    masks = [sub == i for i in range(B)]
    T = n // LANES

    def chain(k, p):
        t0, l0 = (B * k) // LANES, (B * k) % LANES
        c = [jnp.broadcast_to(p[t0][:, l0 + j:l0 + j + 1], (B, LANES)) for j in range(B)]
        p = list(p)
        for i in range(B):
            inv = recip(c[i][i:i + 1, :])
            ci = c[i]
            for j in range(B):
                if j == i:
                    c[j] = jnp.where(masks[i], inv, -ci * inv)
                else:
                    t = c[j][i:i + 1, :] * inv
                    c[j] = jnp.where(masks[i], t, c[j] - ci * t)
            for v in range(T + 1):
                r = p[v][i:i + 1, :] * inv
                p[v] = jnp.where(masks[i], r, p[v] - ci * r)
        dinv = jnp.zeros((B, LANES), F32)
        for j in range(B):
            dinv = jnp.where(lane == l0 + j, c[j], dinv)
        inside = (lane >= l0) & (lane < l0 + B)
        ident = jnp.where(lane == l0 + sub, 1.0, 0.0)
        x, xs = list(p), list(p)
        x[t0] = jnp.where(inside, ident - dinv, p[t0])
        xs[t0] = jnp.where(inside, -dinv, p[t0])
        return x, xs

    def stack(p, x):
        ph, pm, pl_ = split3(p)
        xh, xm, xl = split3(x)
        join = lambda *parts: jnp.concatenate([q.astype(F32) for q in parts], axis=0).astype(BF)
        return join(ph, ph, pm, ph, pl_, pm), join(xh, xm, xh, xl, xh, xm)

    cat = lambda v: jnp.concatenate(v, axis=1)
    tn = (((0,), (0,)), ((), ()))
    p = [W[0:B, v * LANES:(v + 1) * LANES] for v in range(T + 1)]
    old = None
    for k in range(n // B):
        if old is not None:
            po, xo, xso = old
            ps, xs = stack(cat(po[:T]), cat(xo))
            W[...] = W[...] - lax.dot_general(ps, xs, tn, preferred_element_type=F32)
            W[B * (k - 1):B * k, :] = cat(xso)
        x, xs = chain(k, p)
        old = (p, x, xs)
        if k + 1 < n // B:
            nxt = [W[B * (k + 1):B * (k + 2), v * LANES:(v + 1) * LANES] for v in range(T + 1)]
            t0, l0 = (B * k) // LANES, (B * k) % LANES
            cols = [nxt[t0][:, l0 + i:l0 + i + 1] for i in range(B)]
            for v in range(T + 1):
                terms = [cols[i] * x[v][i:i + 1, :] for i in range(B)]
                while len(terms) > 1:
                    terms = [terms[q] + terms[q + 1] for q in range(0, len(terms), 2)]
                nxt[v] = nxt[v] - terms[0]
            p = nxt
    po, xo, xso = old
    ps, xs = stack(cat(po[:T]), xo[T])
    return W[:, n:] - lax.dot_general(ps, xs, tn, preferred_element_type=F32), xso[T]


def prepare(spin, acts, cot, embed, energy_ref, stage, cstage, lin, cin):
    for t in range(TOKS):
        stage[2 * t:2 * t + 2, :] = acts[t].astype(F32)
        cstage[2 * t:2 * t + 2, :] = cot[t].astype(F32)
    sub = lax.broadcasted_iota(jnp.int32, (ROWS2, SITES), 0)
    site = lax.broadcasted_iota(jnp.int32, (ROWS2, SITES), 1)
    spins = spin[...].astype(F32)
    patches = jnp.where(sub % 2 == 0, spins[0:1, :], spins[1:2, :])
    patches = jnp.where(site // PATCH == sub // 2, patches, 0.0).astype(BF)
    turn = lax.broadcasted_iota(jnp.int32, (SITES, WIDTH), 0) % PATCH
    table = embed[...].astype(F32)
    spread = jnp.zeros((SITES, WIDTH), F32)
    for k in range(PATCH):
        spread = jnp.where(turn == k, table[k:k + 1, :], spread)
    added = jnp.dot(patches, spread.astype(BF), preferred_element_type=F32)
    stage[:ROWS2, :] = (stage[:ROWS2, :] + added).astype(BF).astype(F32)
    stage[ROWS2:, :] = jnp.zeros((LANES - ROWS2, WIDTH), F32)
    for v in range(WIDTH // LANES):
        lin[v * LANES:(v + 1) * LANES, :] = stage[:, v * LANES:(v + 1) * LANES].T.astype(BF)
    lane = lax.broadcasted_iota(jnp.int32, (ROWS2, LANES), 1)
    row = lax.broadcasted_iota(jnp.int32, (ROWS2, LANES), 0)
    energy = jnp.where(lane < JB + 3, jnp.full((ROWS2, LANES), energy_ref[0], F32), jnp.full((ROWS2, LANES), energy_ref[1], F32))
    high, mid, low = (t.astype(F32) for t in split3(energy))
    third = lane % 3
    parts = jnp.where(third == 0, high, jnp.where(third == 1, mid, low))
    parts = jnp.where((row == 0) & (lane < JB + 6), parts, 0.0)
    for b in range(8):
        t, o = (JB * b) // LANES, (JB * b) % LANES
        piece = cstage[:, t * LANES:(t + 1) * LANES]
        if o:
            piece = pltpu.roll(piece, LANES - o, 1)
            if LANES - o < JB:
                after = pltpu.roll(cstage[:, (t + 1) * LANES:(t + 2) * LANES], LANES - o, 1)
                piece = jnp.where(lane < LANES - o, piece, after)
        cin[b] = jnp.where(lane < JB, piece, parts).astype(BF)


def main_kernel(energy_ref, damp_ref, spin_hbm, acts_hbm, cot_hbm, embed_hbm, slot_hbm, out_ref,
                spin_v, acts_v, cot_v, embed_v, slot_ref, in_sem, stage, cstage, lin_ref, cin_ref,
                gt, erow_ref, cen_ref, W, wv, upd, ur, f_s, f_r,
                lraw, lpk, call, rbuf, esc, gacc, gp, cbuf, rr, s1, cr, s2,
                l1s, l1r, c1s, c1r, c2s, c2r, c3s, c3r, l2s, l2r,
                a_s, a_r, b_s, b_r, x_s, x_r, d_s, d_r, e_s, e_r):
    g, d, x_hi, core, z, rb = place()
    a = g * 4 + z
    b = flip(rb, x_hi)
    q, y = b % 2, b // 2
    partner = (x_hi * 2 + 1 - core, d)

    def cpos(du, dv, other=0):
        c = core + other * (1 - 2 * core)
        return (((x_hi + du) % 2) * 2 + c) * 4 + (z + dv) % 4

    def lpos(du, dv):
        return ((y + dv) % 4) * 2 + (q + du) % 2

    barrier = pltpu.get_barrier_semaphore()
    for k in range(1, 16):
        pl.semaphore_signal(barrier, inc=1, device_id=column_device((a + k) % 16, b), device_id_type=MESH)
    for k in range(1, 8):
        pl.semaphore_signal(barrier, inc=1, device_id=column_device(a, (b + k) % 8), device_id_type=MESH)
    loads = [pltpu.make_async_copy(src, dst, in_sem.at[n]) for n, (src, dst) in enumerate(
        ((spin_hbm, spin_v), (acts_hbm, acts_v), (cot_hbm, cot_v), (embed_hbm, embed_v), (slot_hbm, slot_ref)))]
    for copy in loads:
        copy.start()
    for copy in loads:
        copy.wait()
    prepare(spin_v, acts_v, cot_v, embed_v, energy_ref, stage, cstage, lin_ref, cin_ref)
    pl.semaphore_wait(barrier, 22)

    sends = []

    def start(copy):
        copy.start()
        sends.append(copy)

    def arrived(ref, sem):
        remote(ref, ref, sem, sem, partner).wait_recv()

    others = ((1, 2), (0, 2), (1, 1), (1, 3), (0, 1), (0, 3), (1, 0))
    for k, org in enumerate(others):
        bt = lpos(*org)
        start(remote(cin_ref.at[bt], call.at[a, b], c1s.at[k], c1r.at[b], column_device(a, bt)))
    for k, (org, other) in enumerate([(org, other) for org in others for other in range(2)] + [((0, 0), 1)]):
        at = cpos(*org, other)
        start(remote(lin_ref.at[pl.ds(pl.multiple_of(at * IB, IB), IB)], lraw.at[a], l1s.at[k], l1r.at[a], column_device(at, b)))
    call[a, b] = cin_ref[b]
    lraw[a] = lin_ref[pl.ds(pl.multiple_of(a * IB, IB), IB), :]

    def chalf(p, h):
        return call.at[p] if h is None else call.at[p, pl.ds(4 * h, 4)]

    def lhalf(p, h):
        return lpk.at[p] if h is None else lpk.at[p, pl.ds(5 * h, 5 - h)]

    slot_c, slot_l = [0], [0]

    def csend(org, h, to, seen):
        ref = chalf(cpos(*org), h)
        start(remote(ref, ref, c2s.at[slot_c[0]], c2r.at[seen[0] * 4 + seen[1], h or 0], column_device(cpos(*to), b)))
        slot_c[0] += 1

    def lsend(org, h, to, seen):
        ref = lhalf(lpos(*org), h)
        start(remote(ref, ref, l2s.at[slot_l[0]], l2r.at[seen[0] * 4 + seen[1], h or 0], column_device(a, lpos(*to))))
        slot_l[0] += 1

    def over(org, h=None):
        ref = chalf(cpos(*org), h)
        n = org[0] * 4 + org[1]
        start(remote(ref, ref, c3s.at[n, h or 0], c3r.at[n, h or 0], partner))

    def cwait(org, h=None):
        arrived(chalf(cpos(*org), h), c2r.at[org[0] * 4 + org[1], h or 0])

    def owait(org, h=None):
        arrived(chalf(cpos(*org, 1), h), c3r.at[org[0] * 4 + org[1], h or 0])

    def lwait(org, h=None):
        arrived(lhalf(lpos(*org), h), l2r.at[org[0] * 4 + org[1], h or 0])

    HERE, PAIR, UP, DOWN = (0, 0), (1, 0), (0, 1), (0, 3)

    for k in range(1, 8):
        bs = (b + 8 - k) % 8
        arrived(call.at[a, bs], c1r.at[bs])
    csend(HERE, None, PAIR, (1, 0))
    csend(HERE, None, UP, (0, 3))
    csend(HERE, None, DOWN, (0, 1))
    over(HERE)

    for k in range(1, 16):
        asrc = (a + 16 - k) % 16
        arrived(lraw.at[asrc], l1r.at[asrc])
    packed = jnp.concatenate([lraw[s][:, :ROWS2] for s in range(16)], axis=1)
    for t in range(9):
        lpk[b, t] = packed[:, t * LANES:(t + 1) * LANES]
    lsend(HERE, None, PAIR, (1, 0))
    lsend(HERE, None, UP, (0, 3))
    lsend(HERE, None, DOWN, (0, 1))

    cwait(PAIR)
    csend(PAIR, 1, UP, (1, 3))
    csend(PAIR, 1, DOWN, (1, 1))
    over(PAIR)
    lwait(PAIR)
    lsend(PAIR, 1, UP, (1, 3))
    lsend(PAIR, 1, DOWN, (1, 1))
    cwait((0, 3))
    csend((0, 3), 0, UP, (0, 2))
    csend((0, 3), 0, PAIR, (1, 3))
    over((0, 3))
    cwait((0, 1))
    csend((0, 1), 1, DOWN, (0, 2))
    csend((0, 1), 0, PAIR, (1, 1))
    over((0, 1))
    lwait((0, 3))
    lsend((0, 3), 0, UP, (0, 2))
    lsend((0, 3), 0, PAIR, (1, 3))
    lwait((0, 1))
    lsend((0, 1), 1, DOWN, (0, 2))
    lsend((0, 1), 0, PAIR, (1, 1))
    for org, h, to in (((1, 3), 0, UP), ((1, 1), 1, DOWN)):
        cwait(org, h)
        csend(org, h, to, (1, 2))
        over(org, h)
        lwait(org, h)
        lsend(org, h, to, (1, 2))
    for org, h in (((1, 3), 1), ((1, 1), 0)):
        cwait(org, h)
        over(org, h)
        lwait(org, h)

    lane = lax.broadcasted_iota(jnp.int32, (IB, LANES), 1)
    first = jnp.where((lane % 2 == 0) & (lane < ROWS2), 1.0, 0.0)
    second = jnp.where((lane % 2 == 1) & (lane < ROWS2), 1.0, 0.0)
    lane1 = lax.broadcasted_iota(jnp.int32, (1, LANES), 1)
    scale = jnp.where(lane1 < JB, 1.0 / math.sqrt(TOKS), 0.0)

    def rows_of(other, rc, lsteps):
        asrc = cpos(*rel(rc), other)
        off = asrc * ROWS2
        t0 = off // LANES
        o = off % LANES
        t1 = jnp.minimum(t0 + 1, 8)
        shift = (LANES - o) % LANES
        for rl in lsteps:
            bs = lpos(*rel(rl))
            lo = pltpu.roll(lpk[bs, t0].astype(F32), shift, 1)
            hi = pltpu.roll(lpk[bs, t1].astype(F32), shift, 1)
            left = jnp.where(lane < LANES - o, lo, hi)
            left = jnp.concatenate([left * first, left * second], axis=0).astype(BF)
            right = call[asrc, bs]
            prod = lax.dot_general(left[:, :ROWS2], right, (((1,), (0,)), ((), ())), preferred_element_type=F32)
            at = asrc * 8 + flip(bs, asrc // 8)
            rbuf[pl.ds(pl.multiple_of(at * 2 * IB, 2 * IB), 2 * IB), :] = (prod * scale).astype(BF).astype(F32)
            esc[pl.ds(at, 1), :] = right.astype(F32)[0:1, :]

    def rows_loop(other, lo, hi, lsteps):
        def body(rc, carry):
            rows_of(other, rc, lsteps)
            return carry
        lax.fori_loop(lo, hi, body, 0)

    rows_loop(0, 0, 6, range(6))
    for org in (HERE, PAIR, DOWN, UP):
        owait(org)
    for org, h in (((1, 3), 0), ((1, 1), 1), ((1, 3), 1), ((1, 1), 0)):
        owait(org, h)
    rows_loop(1, 0, 6, range(6))
    for u in range(2):
        for h in range(2):
            cwait((u, 2), h)
            over((u, 2), h)
        for h in range(2):
            lwait((u, 2), h)
    for other in range(2):
        rows_loop(other, 0, 6, range(6, 8))
    rows_loop(0, 6, 8, range(8))
    for u in range(2):
        for h in range(2):
            owait((u, 2), h)
    rows_loop(1, 6, 8, range(8))

    gacc[...] = jnp.zeros_like(gacc)
    inv_root = 1.0 / math.sqrt(WIDTH * WIDTH)

    def gram_step(m, carry):
        xs = [rbuf[pl.ds(pl.multiple_of(s * IB + m * 8, 8), 8), :] for s in range(SLOTS)]
        sums = xs[:8]
        for s in range(8, SLOTS):
            sums[s % 8] = sums[s % 8] + xs[s]
        while len(sums) > 1:
            sums = [sums[n] + sums[n + 1] for n in range(0, len(sums), 2)]
        mean = sums[0] * (1.0 / SLOTS)
        c = jnp.concatenate([((x - mean) * inv_root)[None] for x in xs], axis=0)
        c = jnp.transpose(c, (1, 0, 2)).astype(BF)
        cen_ref[pl.ds(pl.multiple_of(m * 8, 8), 8)] = c
        c = jnp.concatenate([c[n] for n in range(8)], axis=1)
        gacc[...] += lax.dot_general(c, c, (((1,), (1,)), ((), ())), preferred_element_type=F32)
        return carry

    lax.fori_loop(0, IB // 8, gram_step, 0)

    for t in range(48):
        blk, w = t // 16, t % 16
        r0 = (0, 128, 128)[blk] + 8 * w
        c0 = (0, 0, 128)[blk]
        gp[t // 24, (t % 24) // 3, t % 3] = gacc[r0:r0 + 8, c0:c0 + 128]

    start(remote(gp.at[1 - core], cbuf, a_s, a_r, partner))
    arrived(cbuf, a_r)
    cbuf[...] = cbuf[...] + gp[core]
    for k, org in enumerate(others):
        bt = lpos(*org)
        start(remote(cbuf.at[bt], rr.at[b], b_s.at[k], b_r.at[b], column_device(a, bt)))
    rr[b] = cbuf[b]

    parts = esc[...]
    pos = lax.broadcasted_iota(jnp.int32, (LANES, LANES), 0) * 2
    for half in range(2):
        row = jnp.zeros((1, LANES), F32)
        for k in range(2):
            e = parts[:, JB + 3 * k:JB + 3 * k + 1] + parts[:, JB + 3 * k + 1:JB + 3 * k + 2] + parts[:, JB + 3 * k + 2:JB + 3 * k + 3]
            hit = slot_ref[half:half + 1, :] == pos + k
            row = row + jnp.sum(jnp.where(hit, e, 0.0), axis=0, keepdims=True)
        erow_ref[half:half + 1, :] = row

    e_row = jnp.concatenate([erow_ref[0:1, :], erow_ref[1:2, :]], axis=1)
    sh = e_row - jnp.sum(e_row, axis=1, keepdims=True) * (1.0 / SLOTS)
    rows = lax.broadcasted_iota(jnp.int32, (SLOTS, SLOTS), 0)
    cols = lax.broadcasted_iota(jnp.int32, (SLOTS, SLOTS), 1)
    eye = rows == cols
    W[:, SLOTS:] = jnp.broadcast_to(jnp.sum(jnp.where(eye, sh, 0.0), axis=1, keepdims=True), (SLOTS, LANES))

    for k in range(1, 8):
        bs = (b + 8 - k) % 8
        arrived(rr.at[bs], b_r.at[bs])
    total = rr[0]
    for k in range(1, 8):
        total = total + rr[k]
    s1[...] = total
    chip = x_hi * 4 + z
    cr[chip] = total
    for k, org in enumerate(others):
        start(remote(s1, cr.at[chip], x_s.at[k], x_r.at[chip], column_device(cpos(*org), b)))
    for k in range(1, 8):
        cs = (chip + 8 - k) % 8
        arrived(cr.at[cs], x_r.at[cs])
    total = cr[0]
    for k in range(1, 8):
        total = total + cr[k]
    s2[...] = total
    gt[core, b] = total
    for k, org in enumerate(others):
        start(remote(s2, gt.at[core, b], d_s.at[k], d_r.at[b], column_device(a, lpos(*org))))
    start(remote(s2, gt.at[core, b], e_s.at[0], e_r.at[b], partner))
    for k, org in zip(range(1, 8), others[::-1]):
        bs = lpos(*org)
        arrived(gt.at[core, bs], d_r.at[bs])
        start(remote(gt.at[core, bs], gt.at[core, bs], e_s.at[k], e_r.at[bs], partner))
    for k in range(8):
        bs = (b + 8 - k) % 8
        arrived(gt.at[1 - core, bs], e_r.at[bs])

    for t in range(48):
        blk, w = t // 16, t % 16
        r0 = (0, 128, 128)[blk] + 8 * w
        c0 = (0, 0, 128)[blk]
        W[r0:r0 + 8, c0:c0 + 128] = gt[t // 24, (t % 24) // 3, t % 3]
    W[0:128, 128:256] = W[128:256, 0:128].T
    W[:, 0:SLOTS] = W[:, 0:SLOTS] + jnp.where(eye, damp_ref[0], 0.0)
    weights, last = sweep(W, SLOTS, 8)
    wv[...] = weights
    wv[SLOTS - 8:, :] = last

    step_scale = -math.sqrt(WIDTH * WIDTH / SLOTS)

    def update_rows(r):
        done = []
        for v in range(6):
            c = cen_ref[r * 6 + v].astype(F32)
            done.append(jnp.sum(c * wv[...], axis=0, keepdims=True) * step_scale)
        done.append(jnp.zeros((2, LANES), F32))
        upd[r] = jnp.concatenate(done, axis=0)

    for k, org in enumerate(others):
        bt = lpos(*org)
        update_rows(flip(bt, x_hi))
        start(remote(upd.at[flip(bt, x_hi)], ur.at[b], f_s.at[k], f_r.at[b], column_device(a, bt)))
    update_rows(rb)
    ur[b] = upd[rb]
    for copy in sends[:-7]:
        copy.wait_send()
    for k in range(1, 8):
        bs = (b + 8 - k) % 8
        arrived(ur.at[bs], f_r.at[bs])
    whole = jnp.concatenate([ur[n][:, :JB] for n in range(8)], axis=1)
    for i in range(6):
        for v in range(6):
            out_ref[6 * i + v:6 * i + v + 1, :] = whole[i:i + 1, v * LANES:(v + 1) * LANES]
    for copy in sends[-7:]:
        copy.wait_send()


def main_call(energies, damping, spin, acts, cot, embed, slots):
    dma = pltpu.SemaphoreType.DMA
    smem = pl.BlockSpec(memory_space=pltpu.SMEM)
    hbm = pl.BlockSpec(memory_space=pl.ANY)
    return pl.pallas_call(
        main_kernel,
        out_shape=jax.ShapeDtypeStruct((36, LANES), F32),
        in_specs=[smem, smem, hbm, hbm, hbm, hbm, hbm],
        out_specs=pl.BlockSpec(memory_space=pltpu.VMEM),
        scratch_shapes=[
            pltpu.VMEM(spin.shape, jnp.int32),
            pltpu.VMEM(acts.shape, BF),
            pltpu.VMEM(cot.shape, BF),
            pltpu.VMEM(embed.shape, BF),
            pltpu.VMEM(slots.shape, jnp.int32),
            dma((5,)),
            pltpu.VMEM((LANES, WIDTH), F32),
            pltpu.VMEM((ROWS2, WIDTH), F32),
            pltpu.VMEM((WIDTH, LANES), BF),
            pltpu.VMEM((8, ROWS2, LANES), BF),
            pltpu.VMEM((2, 8, 3, 8, LANES), F32),
            pltpu.VMEM((2, LANES), F32),
            pltpu.VMEM((IB, SLOTS, LANES), BF),
            pltpu.VMEM((SLOTS, SLOTS + LANES), F32),
            pltpu.VMEM((SLOTS, LANES), F32),
            pltpu.VMEM((8, 8, LANES), F32),
            pltpu.VMEM((8, 8, LANES), F32),
            dma((8,)), dma((8,)),
            pltpu.VMEM((16, IB, LANES), BF),
            pltpu.VMEM((8, 9, IB, LANES), BF),
            pltpu.VMEM((16, 8, ROWS2, LANES), BF),
            pltpu.VMEM((SLOTS * IB, LANES), F32),
            pltpu.VMEM((LANES, LANES), F32),
            pltpu.VMEM((SLOTS, SLOTS), F32),
            pltpu.VMEM((2, 8, 3, 8, LANES), F32),
            pltpu.VMEM((8, 3, 8, LANES), F32),
            pltpu.VMEM((8, 3, 8, LANES), F32),
            pltpu.VMEM((3, 8, LANES), F32),
            pltpu.VMEM((8, 3, 8, LANES), F32),
            pltpu.VMEM((3, 8, LANES), F32),
            dma((16,)), dma((16,)), dma((8,)), dma((8,)), dma((11,)), dma((8, 2)),
            dma((8, 2)), dma((8, 2)), dma((11,)), dma((8, 2)),
            dma(()), dma(()), dma((8,)), dma((8,)), dma((8,)), dma((8,)), dma((8,)), dma((8,)), dma((8,)), dma((8,)),
        ],
        compiler_params=pltpu.CompilerParams(
            collective_id=0, has_side_effects=True, vmem_limit_bytes=60000000),
        name="main",
    )(energies, damping, spin, acts, cot, embed, slots)


def shards(spin_config, layer_acts, cotangent, patch_embed, energies, slot_sample, damping):
    out = main_call(energies, damping.reshape(1), spin_config, layer_acts.transpose(1, 0, 2),
                    cotangent.transpose(1, 0, 2), patch_embed,
                    slot_sample.reshape(2, LANES))
    return out.reshape(-1)


def solution(mesh):
    return jax.shard_map(
        shards,
        mesh=mesh,
        in_specs=(
            P(("grp", "dev"), None),
            P(("grp", "dev"), None, None),
            P(("grp", "dev"), None, None),
            P(),
            P(("grp", "dev")),
            P(),
            P(),
        ),
        out_specs=P(("grp", "dev")),
        check_vma=False,
    )
```

```python
import math

import jax
import jax.numpy as jnp
from jax import lax
from jax.experimental import pallas as pl
from jax.experimental.pallas import tpu as pltpu
from jax.sharding import PartitionSpec as P

F32 = jnp.float32
BF = jnp.bfloat16
MESH = pl.DeviceIdType.MESH
SLOTS = 256
WIDTH = 768
SITES = 144
PATCH = 4
TOKS = 36
IB = 48
JB = 96
ROWS2 = 2 * TOKS
LANES = 128


def flip(index, high):
    return index + high * (1 - 2 * (index % 2))


def place():
    g = lax.axis_index("grp")
    d = lax.axis_index("dev")
    x_hi, core = g // 2, g % 2
    z, rb = d // 8, d % 8
    return g, d, x_hi, core, z, rb


def column_device(a, b):
    g, z = a // 4, a % 4
    return (g, z * 8 + flip(b, g // 2))


def remote(src, dst, send_sem, recv_sem, device):
    return pltpu.make_async_remote_copy(
        src_ref=src, dst_ref=dst, send_sem=send_sem, recv_sem=recv_sem,
        device_id=device, device_id_type=MESH,
    )


def rel(r):
    m = r // 2
    return r % 2, m + (m // 2) * (1 - 2 * (m % 2))


def split3(x):
    high = x.astype(BF)
    rest = x - high.astype(F32)
    mid = rest.astype(BF)
    return high, mid, (rest - mid.astype(F32)).astype(BF)


def recip(x):
    r = pl.reciprocal(x, approx=True)
    return r * (2.0 - x * r)


def sweep(W, n, B):
    sub = lax.broadcasted_iota(jnp.int32, (B, LANES), 0)
    lane = lax.broadcasted_iota(jnp.int32, (B, LANES), 1)
    masks = [sub == i for i in range(B)]
    T = n // LANES

    def chain(k, p):
        t0, l0 = (B * k) // LANES, (B * k) % LANES
        c = [jnp.broadcast_to(p[t0][:, l0 + j:l0 + j + 1], (B, LANES)) for j in range(B)]
        p = list(p)
        for i in range(B):
            inv = recip(c[i][i:i + 1, :])
            ci = c[i]
            for j in range(B):
                if j == i:
                    c[j] = jnp.where(masks[i], inv, -ci * inv)
                else:
                    t = c[j][i:i + 1, :] * inv
                    c[j] = jnp.where(masks[i], t, c[j] - ci * t)
            for v in range(T + 1):
                r = p[v][i:i + 1, :] * inv
                p[v] = jnp.where(masks[i], r, p[v] - ci * r)
        dinv = jnp.zeros((B, LANES), F32)
        for j in range(B):
            dinv = jnp.where(lane == l0 + j, c[j], dinv)
        inside = (lane >= l0) & (lane < l0 + B)
        ident = jnp.where(lane == l0 + sub, 1.0, 0.0)
        x, xs = list(p), list(p)
        x[t0] = jnp.where(inside, ident - dinv, p[t0])
        xs[t0] = jnp.where(inside, -dinv, p[t0])
        return x, xs

    def stack(p, x):
        ph, pm, pl_ = split3(p)
        xh, xm, xl = split3(x)
        join = lambda *parts: jnp.concatenate([q.astype(F32) for q in parts], axis=0).astype(BF)
        return join(ph, ph, pm, ph, pl_, pm), join(xh, xm, xh, xl, xh, xm)

    cat = lambda v: jnp.concatenate(v, axis=1)
    tn = (((0,), (0,)), ((), ()))
    p = [W[0:B, v * LANES:(v + 1) * LANES] for v in range(T + 1)]
    old = None
    for k in range(n // B):
        if old is not None:
            po, xo, xso = old
            ps, xs = stack(cat(po[:T]), cat(xo))
            W[...] = W[...] - lax.dot_general(ps, xs, tn, preferred_element_type=F32)
            W[B * (k - 1):B * k, :] = cat(xso)
        x, xs = chain(k, p)
        old = (p, x, xs)
        if k + 1 < n // B:
            nxt = [W[B * (k + 1):B * (k + 2), v * LANES:(v + 1) * LANES] for v in range(T + 1)]
            t0, l0 = (B * k) // LANES, (B * k) % LANES
            cols = [nxt[t0][:, l0 + i:l0 + i + 1] for i in range(B)]
            for v in range(T + 1):
                terms = [cols[i] * x[v][i:i + 1, :] for i in range(B)]
                while len(terms) > 1:
                    terms = [terms[q] + terms[q + 1] for q in range(0, len(terms), 2)]
                nxt[v] = nxt[v] - terms[0]
            p = nxt
    po, xo, xso = old
    ps, xs = stack(cat(po[:T]), xo[T])
    return W[:, n:] - lax.dot_general(ps, xs, tn, preferred_element_type=F32), xso[T]


def prepare(spin, acts, cot, embed, energy_ref, stage, cstage, lin, cin):
    for t in range(TOKS):
        stage[2 * t:2 * t + 2, :] = acts[t].astype(F32)
        cstage[2 * t:2 * t + 2, :] = cot[t].astype(F32)
    sub = lax.broadcasted_iota(jnp.int32, (ROWS2, SITES), 0)
    site = lax.broadcasted_iota(jnp.int32, (ROWS2, SITES), 1)
    spins = spin[...].astype(F32)
    patches = jnp.where(sub % 2 == 0, spins[0:1, :], spins[1:2, :])
    patches = jnp.where(site // PATCH == sub // 2, patches, 0.0).astype(BF)
    turn = lax.broadcasted_iota(jnp.int32, (SITES, WIDTH), 0) % PATCH
    table = embed[...].astype(F32)
    spread = jnp.zeros((SITES, WIDTH), F32)
    for k in range(PATCH):
        spread = jnp.where(turn == k, table[k:k + 1, :], spread)
    added = jnp.dot(patches, spread.astype(BF), preferred_element_type=F32)
    stage[:ROWS2, :] = (stage[:ROWS2, :] + added).astype(BF).astype(F32)
    stage[ROWS2:, :] = jnp.zeros((LANES - ROWS2, WIDTH), F32)
    for v in range(WIDTH // LANES):
        lin[v * LANES:(v + 1) * LANES, :] = stage[:, v * LANES:(v + 1) * LANES].T.astype(BF)
    lane = lax.broadcasted_iota(jnp.int32, (ROWS2, LANES), 1)
    row = lax.broadcasted_iota(jnp.int32, (ROWS2, LANES), 0)
    energy = jnp.where(lane < JB + 3, jnp.full((ROWS2, LANES), energy_ref[0], F32), jnp.full((ROWS2, LANES), energy_ref[1], F32))
    high, mid, low = (t.astype(F32) for t in split3(energy))
    third = lane % 3
    parts = jnp.where(third == 0, high, jnp.where(third == 1, mid, low))
    parts = jnp.where((row == 0) & (lane < JB + 6), parts, 0.0)
    for b in range(8):
        t, o = (JB * b) // LANES, (JB * b) % LANES
        piece = cstage[:, t * LANES:(t + 1) * LANES]
        if o:
            piece = pltpu.roll(piece, LANES - o, 1)
            if LANES - o < JB:
                after = pltpu.roll(cstage[:, (t + 1) * LANES:(t + 2) * LANES], LANES - o, 1)
                piece = jnp.where(lane < LANES - o, piece, after)
        cin[b] = jnp.where(lane < JB, piece, parts).astype(BF)


def main_kernel(energy_ref, damp_ref, spin_hbm, acts_hbm, cot_hbm, embed_hbm, slot_hbm, out_ref,
                spin_v, acts_v, cot_v, embed_v, slot_ref, in_sem, stage, cstage, lin_ref, cin_ref,
                gt, erow_ref, cen_ref, W, wv, upd, ur, f_s, f_r,
                lraw, lpk, lall, call, rbuf, esc, gacc, gp, cbuf, rr, s1, cr, s2,
                l1s, l1r, c1s, c1r, c2s, c2r, c3s, c3r, l2s, l2r,
                a_s, a_r, b_s, b_r, x_s, x_r, d_s, d_r, e_s, e_r):
    g, d, x_hi, core, z, rb = place()
    a = g * 4 + z
    b = flip(rb, x_hi)
    q, y = b % 2, b // 2
    partner = (x_hi * 2 + 1 - core, d)

    def cpos(du, dv, other=0):
        c = core + other * (1 - 2 * core)
        return (((x_hi + du) % 2) * 2 + c) * 4 + (z + dv) % 4

    def lpos(du, dv):
        return ((y + dv) % 4) * 2 + (q + du) % 2

    barrier = pltpu.get_barrier_semaphore()
    for k in range(1, 16):
        pl.semaphore_signal(barrier, inc=1, device_id=column_device((a + k) % 16, b), device_id_type=MESH)
    for k in range(1, 8):
        pl.semaphore_signal(barrier, inc=1, device_id=column_device(a, (b + k) % 8), device_id_type=MESH)
    across = (1 - 2 * core) * 4
    for k in range(1, 8):
        pl.semaphore_signal(barrier, inc=1, device_id=column_device(a + across, (b + k) % 8), device_id_type=MESH)
    loads = [pltpu.make_async_copy(src, dst, in_sem.at[n]) for n, (src, dst) in enumerate(
        ((spin_hbm, spin_v), (acts_hbm, acts_v), (cot_hbm, cot_v), (embed_hbm, embed_v), (slot_hbm, slot_ref)))]
    for copy in loads:
        copy.start()
    for copy in loads:
        copy.wait()
    prepare(spin_v, acts_v, cot_v, embed_v, energy_ref, stage, cstage, lin_ref, cin_ref)
    pl.semaphore_wait(barrier, 29)

    sends = []

    def start(copy):
        copy.start()
        sends.append(copy)

    def arrived(ref, sem):
        remote(ref, ref, sem, sem, partner).wait_recv()

    others = ((1, 2), (0, 2), (1, 1), (1, 3), (0, 1), (0, 3), (1, 0))
    for k, org in enumerate(others):
        bt = lpos(*org)
        start(remote(cin_ref.at[bt], call.at[a, b], c1s.at[k], c1r.at[b], column_device(a, bt)))
    for k, (org, other) in enumerate([(org, other) for org in others for other in range(2)] + [((0, 0), 1)]):
        at = cpos(*org, other)
        start(remote(lin_ref.at[pl.ds(pl.multiple_of(at * IB, IB), IB)], lraw.at[a], l1s.at[k], l1r.at[a], column_device(at, b)))
    call[a, b] = cin_ref[b]
    lraw[a] = lin_ref[pl.ds(pl.multiple_of(a * IB, IB), IB), :]

    def chalf(p, h):
        return call.at[p] if h is None else call.at[p, pl.ds(4 * h, 4)]

    def lhalf(p, h):
        return lpk.at[p] if h is None else lpk.at[p, pl.ds(5 * h, 5 - h)]

    slot_c, slot_l = [0], [0]

    def csend(org, h, to, seen):
        ref = chalf(cpos(*org), h)
        start(remote(ref, ref, c2s.at[slot_c[0]], c2r.at[seen[0] * 4 + seen[1], h or 0], column_device(cpos(*to), b)))
        slot_c[0] += 1

    def lsend(org, h, to, seen):
        ref = lhalf(lpos(*org), h)
        start(remote(ref, ref, l2s.at[slot_l[0]], l2r.at[seen[0] * 4 + seen[1], h or 0], column_device(a, lpos(*to))))
        slot_l[0] += 1

    def over(org, h=None):
        ref = chalf(cpos(*org), h)
        n = org[0] * 4 + org[1]
        start(remote(ref, ref, c3s.at[n, h or 0], c3r.at[n, h or 0], partner))

    def cwait(org, h=None):
        arrived(chalf(cpos(*org), h), c2r.at[org[0] * 4 + org[1], h or 0])

    def owait(org, h=None):
        arrived(chalf(cpos(*org, 1), h), c3r.at[org[0] * 4 + org[1], h or 0])

    def lwait(org, h=None):
        arrived(lhalf(lpos(*org), h), l2r.at[org[0] * 4 + org[1], h or 0])

    HERE, PAIR, UP, DOWN = (0, 0), (1, 0), (0, 1), (0, 3)
    left_lane = lax.broadcasted_iota(jnp.int32, (IB, LANES), 1)

    def unpack(org):
        bs = lpos(*org)
        for n in range(16):
            t, o = (n * ROWS2) // LANES, (n * ROWS2) % LANES
            tile = lpk[bs, t].astype(F32)
            if o:
                tile = pltpu.roll(tile, LANES - o, 1)
                if LANES - o < ROWS2:
                    tile = jnp.where(left_lane < LANES - o, tile, pltpu.roll(lpk[bs, t + 1].astype(F32), LANES - o, 1))
            lall[bs, n] = tile.astype(BF)

    for k in range(1, 8):
        bs = (b + 8 - k) % 8
        arrived(call.at[a, bs], c1r.at[bs])
    csend(HERE, None, PAIR, (1, 0))
    csend(HERE, None, UP, (0, 3))
    csend(HERE, None, DOWN, (0, 1))
    over(HERE)

    for k in range(1, 16):
        asrc = (a + 16 - k) % 16
        arrived(lraw.at[asrc], l1r.at[asrc])
    packed = jnp.concatenate([lraw[s][:, :ROWS2] for s in range(16)], axis=1)
    for t in range(9):
        lpk[b, t] = packed[:, t * LANES:(t + 1) * LANES]
    lsend(HERE, None, PAIR, (1, 0))
    lsend(HERE, None, UP, (0, 3))
    lsend(HERE, None, DOWN, (0, 1))

    cwait(PAIR)
    csend(PAIR, 1, UP, (1, 3))
    csend(PAIR, 1, DOWN, (1, 1))
    over(PAIR)
    lwait(PAIR)
    lsend(PAIR, 1, UP, (1, 3))
    lsend(PAIR, 1, DOWN, (1, 1))
    lall[b] = lraw[...]
    unpack(PAIR)
    cwait((0, 3))
    csend((0, 3), 0, UP, (0, 2))
    csend((0, 3), 0, PAIR, (1, 3))
    over((0, 3))
    cwait((0, 1))
    csend((0, 1), 1, DOWN, (0, 2))
    csend((0, 1), 0, PAIR, (1, 1))
    over((0, 1))
    lwait((0, 3))
    lsend((0, 3), 0, UP, (0, 2))
    lsend((0, 3), 0, PAIR, (1, 3))
    lwait((0, 1))
    lsend((0, 1), 1, DOWN, (0, 2))
    lsend((0, 1), 0, PAIR, (1, 1))
    unpack((0, 3))
    unpack((0, 1))
    for org, h, to in (((1, 3), 0, UP), ((1, 1), 1, DOWN)):
        cwait(org, h)
        csend(org, h, to, (1, 2))
        over(org, h)
        lwait(org, h)
        lsend(org, h, to, (1, 2))
    for org, h in (((1, 3), 1), ((1, 1), 0)):
        cwait(org, h)
        over(org, h)
        lwait(org, h)
    unpack((1, 3))
    unpack((1, 1))

    lane = lax.broadcasted_iota(jnp.int32, (IB, LANES), 1)
    first = jnp.where((lane % 2 == 0) & (lane < ROWS2), 1.0, 0.0).astype(BF)
    second = jnp.where((lane % 2 == 1) & (lane < ROWS2), 1.0, 0.0).astype(BF)
    lane1 = lax.broadcasted_iota(jnp.int32, (1, LANES), 1)
    scale = jnp.where(lane1 < JB, 1.0 / math.sqrt(TOKS), 0.0)

    def rows_of(other, rc, lsteps):
        asrc = cpos(*rel(rc), other)
        for rl in lsteps:
            bs = lpos(*rel(rl))
            left = lall[bs, asrc]
            left = jnp.concatenate([left * first, left * second], axis=0)
            right = call[asrc, bs]
            prod = lax.dot_general(left[:, :ROWS2], right, (((1,), (0,)), ((), ())), preferred_element_type=F32)
            at = asrc * 8 + flip(bs, asrc // 8)
            rbuf[pl.ds(pl.multiple_of(at * 2 * IB, 2 * IB), 2 * IB), :] = (prod * scale).astype(BF).astype(F32)
            esc[pl.ds(at, 1), :] = right.astype(F32)[0:1, :]

    def rows_loop(other, lo, hi, lsteps):
        def body(rc, carry):
            rows_of(other, rc, lsteps)
            return carry
        lax.fori_loop(lo, hi, body, 0)

    rows_loop(0, 0, 6, range(6))
    for org in (HERE, PAIR, DOWN, UP):
        owait(org)
    for org, h in (((1, 3), 0), ((1, 1), 1), ((1, 3), 1), ((1, 1), 0)):
        owait(org, h)
    rows_loop(1, 0, 6, range(6))
    for u in range(2):
        for h in range(2):
            cwait((u, 2), h)
            over((u, 2), h)
        for h in range(2):
            lwait((u, 2), h)
        unpack((u, 2))
    for other in range(2):
        rows_loop(other, 0, 6, range(6, 8))
    rows_loop(0, 6, 8, range(8))
    for u in range(2):
        for h in range(2):
            owait((u, 2), h)
    rows_loop(1, 6, 8, range(8))

    gacc[...] = jnp.zeros_like(gacc)
    inv_root = 1.0 / math.sqrt(WIDTH * WIDTH)

    def gram_step(m, carry):
        xs = [rbuf[pl.ds(pl.multiple_of(s * IB + m * 8, 8), 8), :] for s in range(SLOTS)]
        sums = xs[:8]
        for s in range(8, SLOTS):
            sums[s % 8] = sums[s % 8] + xs[s]
        while len(sums) > 1:
            sums = [sums[n] + sums[n + 1] for n in range(0, len(sums), 2)]
        mean = sums[0] * (1.0 / SLOTS)
        c = jnp.concatenate([((x - mean) * inv_root)[None] for x in xs], axis=0)
        c = jnp.transpose(c, (1, 0, 2)).astype(BF)
        cen_ref[pl.ds(pl.multiple_of(m * 8, 8), 8)] = c
        c = jnp.concatenate([c[n] for n in range(8)], axis=1)
        gacc[...] += lax.dot_general(c, c, (((1,), (1,)), ((), ())), preferred_element_type=F32)
        return carry

    lax.fori_loop(0, IB // 8, gram_step, 0)

    for t in range(48):
        blk, w = t // 16, t % 16
        r0 = (0, 128, 128)[blk] + 8 * w
        c0 = (0, 0, 128)[blk]
        gp[t // 24, (t % 24) // 3, t % 3] = gacc[r0:r0 + 8, c0:c0 + 128]

    start(remote(gp.at[1 - core], cbuf, a_s, a_r, partner))
    arrived(cbuf, a_r)
    cbuf[...] = cbuf[...] + gp[core]
    for k, org in enumerate(others):
        bt = lpos(*org)
        start(remote(cbuf.at[bt], rr.at[b], b_s.at[k], b_r.at[b], column_device(a, bt)))
    rr[b] = cbuf[b]

    parts = esc[...]
    pos = lax.broadcasted_iota(jnp.int32, (LANES, LANES), 0) * 2
    for half in range(2):
        row = jnp.zeros((1, LANES), F32)
        for k in range(2):
            e = parts[:, JB + 3 * k:JB + 3 * k + 1] + parts[:, JB + 3 * k + 1:JB + 3 * k + 2] + parts[:, JB + 3 * k + 2:JB + 3 * k + 3]
            hit = slot_ref[half:half + 1, :] == pos + k
            row = row + jnp.sum(jnp.where(hit, e, 0.0), axis=0, keepdims=True)
        erow_ref[half:half + 1, :] = row

    e_row = jnp.concatenate([erow_ref[0:1, :], erow_ref[1:2, :]], axis=1)
    sh = e_row - jnp.sum(e_row, axis=1, keepdims=True) * (1.0 / SLOTS)
    rows = lax.broadcasted_iota(jnp.int32, (SLOTS, SLOTS), 0)
    cols = lax.broadcasted_iota(jnp.int32, (SLOTS, SLOTS), 1)
    eye = rows == cols
    W[:, SLOTS:] = jnp.broadcast_to(jnp.sum(jnp.where(eye, sh, 0.0), axis=1, keepdims=True), (SLOTS, LANES))

    for k in range(1, 8):
        bs = (b + 8 - k) % 8
        arrived(rr.at[bs], b_r.at[bs])
    total = rr[0]
    for k in range(1, 8):
        total = total + rr[k]
    s1[...] = total
    chip = x_hi * 4 + z
    cr[chip] = total
    for k, org in enumerate(others):
        start(remote(s1, cr.at[chip], x_s.at[k], x_r.at[chip], column_device(cpos(*org), b)))
    for k in range(1, 8):
        cs = (chip + 8 - k) % 8
        arrived(cr.at[cs], x_r.at[cs])
    total = cr[0]
    for k in range(1, 8):
        total = total + cr[k]
    s2[...] = total
    gt[core, b] = total
    for k, org in enumerate(others):
        start(remote(s2, gt.at[core, b], d_s.at[k], d_r.at[b], column_device(a, lpos(*org))))
        start(remote(s2, gt.at[core, b], e_s.at[k + 1], e_r.at[b], column_device(a + across, lpos(*org))))
    start(remote(s2, gt.at[core, b], e_s.at[0], e_r.at[b], partner))
    for k in range(1, 8):
        bs = (b + 8 - k) % 8
        arrived(gt.at[core, bs], d_r.at[bs])
    for k in range(8):
        bs = (b + 8 - k) % 8
        arrived(gt.at[1 - core, bs], e_r.at[bs])

    for t in range(48):
        blk, w = t // 16, t % 16
        r0 = (0, 128, 128)[blk] + 8 * w
        c0 = (0, 0, 128)[blk]
        W[r0:r0 + 8, c0:c0 + 128] = gt[t // 24, (t % 24) // 3, t % 3]
    W[0:128, 128:256] = W[128:256, 0:128].T
    W[:, 0:SLOTS] = W[:, 0:SLOTS] + jnp.where(eye, damp_ref[0], 0.0)
    weights, last = sweep(W, SLOTS, 8)
    wv[...] = weights
    wv[SLOTS - 8:, :] = last

    def update_rows(r):
        done = []
        for v in range(6):
            c = cen_ref[r * 6 + v].astype(F32)
            done.append(jnp.sum(c * wv[...], axis=0, keepdims=True))
        done.append(jnp.zeros((2, LANES), F32))
        upd[r] = jnp.concatenate(done, axis=0)

    for k, org in enumerate(others):
        bt = lpos(*org)
        update_rows(flip(bt, x_hi))
        start(remote(upd.at[flip(bt, x_hi)], ur.at[b], f_s.at[k], f_r.at[b], column_device(a, bt)))
    update_rows(rb)
    ur[b] = upd[rb]
    for copy in sends[:-7]:
        copy.wait_send()
    for k in range(1, 8):
        bs = (b + 8 - k) % 8
        arrived(ur.at[bs], f_r.at[bs])
    whole = jnp.concatenate([ur[n][:, :JB] for n in range(8)], axis=1)
    for i in range(6):
        for v in range(6):
            out_ref[6 * i + v:6 * i + v + 1, :] = whole[i:i + 1, v * LANES:(v + 1) * LANES]
    for copy in sends[-7:]:
        copy.wait_send()


def main_call(energies, damping, spin, acts, cot, embed, slots):
    dma = pltpu.SemaphoreType.DMA
    smem = pl.BlockSpec(memory_space=pltpu.SMEM)
    hbm = pl.BlockSpec(memory_space=pl.ANY)
    return pl.pallas_call(
        main_kernel,
        out_shape=jax.ShapeDtypeStruct((36, LANES), F32),
        in_specs=[smem, smem, hbm, hbm, hbm, hbm, hbm],
        out_specs=pl.BlockSpec(memory_space=pltpu.VMEM),
        scratch_shapes=[
            pltpu.VMEM(spin.shape, jnp.int32),
            pltpu.VMEM(acts.shape, BF),
            pltpu.VMEM(cot.shape, BF),
            pltpu.VMEM(embed.shape, BF),
            pltpu.VMEM(slots.shape, jnp.int32),
            dma((5,)),
            pltpu.VMEM((LANES, WIDTH), F32),
            pltpu.VMEM((ROWS2, WIDTH), F32),
            pltpu.VMEM((WIDTH, LANES), BF),
            pltpu.VMEM((8, ROWS2, LANES), BF),
            pltpu.VMEM((2, 8, 3, 8, LANES), F32),
            pltpu.VMEM((2, LANES), F32),
            pltpu.VMEM((IB, SLOTS, LANES), BF),
            pltpu.VMEM((SLOTS, SLOTS + LANES), F32),
            pltpu.VMEM((SLOTS, LANES), F32),
            pltpu.VMEM((8, 8, LANES), F32),
            pltpu.VMEM((8, 8, LANES), F32),
            dma((8,)), dma((8,)),
            pltpu.VMEM((16, IB, LANES), BF),
            pltpu.VMEM((8, 9, IB, LANES), BF),
            pltpu.VMEM((8, 16, IB, LANES), BF),
            pltpu.VMEM((16, 8, ROWS2, LANES), BF),
            pltpu.VMEM((SLOTS * IB, LANES), F32),
            pltpu.VMEM((LANES, LANES), F32),
            pltpu.VMEM((SLOTS, SLOTS), F32),
            pltpu.VMEM((2, 8, 3, 8, LANES), F32),
            pltpu.VMEM((8, 3, 8, LANES), F32),
            pltpu.VMEM((8, 3, 8, LANES), F32),
            pltpu.VMEM((3, 8, LANES), F32),
            pltpu.VMEM((8, 3, 8, LANES), F32),
            pltpu.VMEM((3, 8, LANES), F32),
            dma((16,)), dma((16,)), dma((8,)), dma((8,)), dma((11,)), dma((8, 2)),
            dma((8, 2)), dma((8, 2)), dma((11,)), dma((8, 2)),
            dma(()), dma(()), dma((8,)), dma((8,)), dma((8,)), dma((8,)), dma((8,)), dma((8,)), dma((8,)), dma((8,)),
        ],
        compiler_params=pltpu.CompilerParams(
            collective_id=0, has_side_effects=True, vmem_limit_bytes=60000000),
        name="main",
    )(energies, damping, spin, acts, cot, embed, slots)


def shards(spin_config, layer_acts, cotangent, patch_embed, energies, slot_sample, damping):
    out = main_call(energies, damping.reshape(1), spin_config, layer_acts.transpose(1, 0, 2),
                    cotangent.transpose(1, 0, 2), patch_embed,
                    slot_sample.reshape(2, LANES))
    return (out * -math.sqrt(WIDTH * WIDTH / SLOTS)).reshape(-1)


def solution(mesh):
    return jax.shard_map(
        shards,
        mesh=mesh,
        in_specs=(
            P(("grp", "dev"), None),
            P(("grp", "dev"), None, None),
            P(("grp", "dev"), None, None),
            P(),
            P(("grp", "dev")),
            P(),
            P(),
        ),
        out_specs=P(("grp", "dev")),
        check_vma=False,
    )
```

```python
import math

import jax
import jax.numpy as jnp
from jax import lax
from jax.experimental import pallas as pl
from jax.experimental.pallas import tpu as pltpu
from jax.sharding import PartitionSpec as P

F32 = jnp.float32
BF = jnp.bfloat16
MESH = pl.DeviceIdType.MESH
SLOTS = 256
WIDTH = 768
SITES = 144
PATCH = 4
TOKS = 36
IB = 48
JB = 96
ROWS2 = 2 * TOKS
LANES = 128


def flip(index, high):
    return index + high * (1 - 2 * (index % 2))


def place():
    g = lax.axis_index("grp")
    d = lax.axis_index("dev")
    x_hi, core = g // 2, g % 2
    z, rb = d // 8, d % 8
    return g, d, x_hi, core, z, rb


def column_device(a, b):
    g, z = a // 4, a % 4
    return (g, z * 8 + flip(b, g // 2))


def remote(src, dst, send_sem, recv_sem, device):
    return pltpu.make_async_remote_copy(
        src_ref=src, dst_ref=dst, send_sem=send_sem, recv_sem=recv_sem,
        device_id=device, device_id_type=MESH,
    )


def rel(r):
    m = r // 2
    return r % 2, m + (m // 2) * (1 - 2 * (m % 2))


def split3(x):
    high = x.astype(BF)
    rest = x - high.astype(F32)
    mid = rest.astype(BF)
    return high, mid, (rest - mid.astype(F32)).astype(BF)


def recip(x):
    r = pl.reciprocal(x, approx=True)
    return r * (2.0 - x * r)


def sweep(W, n, B):
    sub = lax.broadcasted_iota(jnp.int32, (B, LANES), 0)
    lane = lax.broadcasted_iota(jnp.int32, (B, LANES), 1)
    masks = [sub == i for i in range(B)]
    T = n // LANES

    def chain(k, p):
        t0, l0 = (B * k) // LANES, (B * k) % LANES
        c = [jnp.broadcast_to(p[t0][:, l0 + j:l0 + j + 1], (B, LANES)) for j in range(B)]
        p = list(p)
        for i in range(B):
            inv = recip(c[i][i:i + 1, :])
            ci = c[i]
            for j in range(B):
                if j == i:
                    c[j] = jnp.where(masks[i], inv, -ci * inv)
                else:
                    t = c[j][i:i + 1, :] * inv
                    c[j] = jnp.where(masks[i], t, c[j] - ci * t)
            for v in range(T + 1):
                r = p[v][i:i + 1, :] * inv
                p[v] = jnp.where(masks[i], r, p[v] - ci * r)
        dinv = jnp.zeros((B, LANES), F32)
        for j in range(B):
            dinv = jnp.where(lane == l0 + j, c[j], dinv)
        inside = (lane >= l0) & (lane < l0 + B)
        ident = jnp.where(lane == l0 + sub, 1.0, 0.0)
        x = list(p)
        x[t0] = jnp.where(inside, ident - dinv, p[t0])
        return x, p[T]

    def stack(p, x):
        ph, pm, pl_ = split3(p)
        xh, xm, xl = split3(x)
        join = lambda *parts: jnp.concatenate([q.astype(F32) for q in parts], axis=0).astype(BF)
        return join(ph, ph, pm, ph, pl_, pm), join(xh, xm, xh, xl, xh, xm)

    cat = lambda v: jnp.concatenate(v, axis=1)
    tn = (((0,), (0,)), ((), ()))
    p = [W[0:B, v * LANES:(v + 1) * LANES] for v in range(T + 1)]
    old = None
    for k in range(n // B):
        if old is not None:
            po, xo, xso = old
            ps, xs = stack(cat(po[:T]), cat(xo))
            r0 = B * (k + 1)
            m0 = LANES if r0 >= LANES else 0
            if r0 < n:
                change = lax.dot_general(ps[:, m0:], xs[:, :n], tn, preferred_element_type=F32)
                W[r0:, :n] = W[r0:, :n] - change[r0 - m0:, :]
            W[:, n:] = W[:, n:] - lax.dot_general(ps, xs[:, n:], tn, preferred_element_type=F32)
            W[B * (k - 1):B * k, n:] = xso
        x, xs = chain(k, p)
        old = (p, x, xs)
        if k + 1 < n // B:
            nxt = [W[B * (k + 1):B * (k + 2), v * LANES:(v + 1) * LANES] for v in range(T + 1)]
            t0, l0 = (B * k) // LANES, (B * k) % LANES
            cols = [nxt[t0][:, l0 + i:l0 + i + 1] for i in range(B)]
            for v in range(T + 1):
                terms = [cols[i] * x[v][i:i + 1, :] for i in range(B)]
                while len(terms) > 1:
                    terms = [terms[q] + terms[q + 1] for q in range(0, len(terms), 2)]
                nxt[v] = nxt[v] - terms[0]
            p = nxt
    po, xo, xso = old
    ps, xs = stack(cat(po[:T]), xo[T])
    return W[:, n:] - lax.dot_general(ps, xs, tn, preferred_element_type=F32), xso


def prepare(spin, acts, cot, embed, energy_ref, stage, cstage, lin, cin):
    for t in range(TOKS):
        stage[2 * t:2 * t + 2, :] = acts[t].astype(F32)
        cstage[2 * t:2 * t + 2, :] = cot[t].astype(F32)
    sub = lax.broadcasted_iota(jnp.int32, (ROWS2, SITES), 0)
    site = lax.broadcasted_iota(jnp.int32, (ROWS2, SITES), 1)
    spins = spin[...].astype(F32)
    patches = jnp.where(sub % 2 == 0, spins[0:1, :], spins[1:2, :])
    patches = jnp.where(site // PATCH == sub // 2, patches, 0.0).astype(BF)
    turn = lax.broadcasted_iota(jnp.int32, (SITES, WIDTH), 0) % PATCH
    table = embed[...].astype(F32)
    spread = jnp.zeros((SITES, WIDTH), F32)
    for k in range(PATCH):
        spread = jnp.where(turn == k, table[k:k + 1, :], spread)
    added = jnp.dot(patches, spread.astype(BF), preferred_element_type=F32)
    stage[:ROWS2, :] = (stage[:ROWS2, :] + added).astype(BF).astype(F32)
    stage[ROWS2:, :] = jnp.zeros((LANES - ROWS2, WIDTH), F32)
    for v in range(WIDTH // LANES):
        lin[v * LANES:(v + 1) * LANES, :] = stage[:, v * LANES:(v + 1) * LANES].T.astype(BF)
    lane = lax.broadcasted_iota(jnp.int32, (ROWS2, LANES), 1)
    row = lax.broadcasted_iota(jnp.int32, (ROWS2, LANES), 0)
    energy = jnp.where(lane < JB + 3, jnp.full((ROWS2, LANES), energy_ref[0], F32), jnp.full((ROWS2, LANES), energy_ref[1], F32))
    high, mid, low = (t.astype(F32) for t in split3(energy))
    third = lane % 3
    parts = jnp.where(third == 0, high, jnp.where(third == 1, mid, low))
    parts = jnp.where((row == 0) & (lane < JB + 6), parts, 0.0)
    for b in range(8):
        t, o = (JB * b) // LANES, (JB * b) % LANES
        piece = cstage[:, t * LANES:(t + 1) * LANES]
        if o:
            piece = pltpu.roll(piece, LANES - o, 1)
            if LANES - o < JB:
                after = pltpu.roll(cstage[:, (t + 1) * LANES:(t + 2) * LANES], LANES - o, 1)
                piece = jnp.where(lane < LANES - o, piece, after)
        cin[b] = jnp.where(lane < JB, piece, parts).astype(BF)


def main_kernel(energy_ref, damp_ref, spin_hbm, acts_hbm, cot_hbm, embed_hbm, slot_hbm, out_ref,
                spin_v, acts_v, cot_v, embed_v, slot_ref, in_sem, stage, cstage, lin_ref, cin_ref,
                gt, erow_ref, cen_ref, W, wv, upd, ur, f_s, f_r,
                lraw, lpk, lall, call, rbuf, esc, gacc, gp, cbuf, rr, s1, cr, s2,
                l1s, l1r, c1s, c1r, c2s, c2r, c3s, c3r, l2s, l2r,
                a_s, a_r, b_s, b_r, x_s, x_r, d_s, d_r, e_s, e_r):
    g, d, x_hi, core, z, rb = place()
    a = g * 4 + z
    b = flip(rb, x_hi)
    q, y = b % 2, b // 2
    partner = (x_hi * 2 + 1 - core, d)

    def cpos(du, dv, other=0):
        c = core + other * (1 - 2 * core)
        return (((x_hi + du) % 2) * 2 + c) * 4 + (z + dv) % 4

    def lpos(du, dv):
        return ((y + dv) % 4) * 2 + (q + du) % 2

    barrier = pltpu.get_barrier_semaphore()
    for k in range(1, 16):
        pl.semaphore_signal(barrier, inc=1, device_id=column_device((a + k) % 16, b), device_id_type=MESH)
    for k in range(1, 8):
        pl.semaphore_signal(barrier, inc=1, device_id=column_device(a, (b + k) % 8), device_id_type=MESH)
    across = (1 - 2 * core) * 4
    for k in range(1, 8):
        pl.semaphore_signal(barrier, inc=1, device_id=column_device(a + across, (b + k) % 8), device_id_type=MESH)
    loads = [pltpu.make_async_copy(src, dst, in_sem.at[n]) for n, (src, dst) in enumerate(
        ((spin_hbm, spin_v), (acts_hbm, acts_v), (cot_hbm, cot_v), (embed_hbm, embed_v), (slot_hbm, slot_ref)))]
    for copy in loads:
        copy.start()
    for copy in loads:
        copy.wait()
    prepare(spin_v, acts_v, cot_v, embed_v, energy_ref, stage, cstage, lin_ref, cin_ref)
    pl.semaphore_wait(barrier, 29)

    sends = []

    def start(copy):
        copy.start()
        sends.append(copy)

    def arrived(ref, sem):
        remote(ref, ref, sem, sem, partner).wait_recv()

    others = ((1, 2), (0, 2), (1, 1), (1, 3), (0, 1), (0, 3), (1, 0))
    for k, org in enumerate(others):
        bt = lpos(*org)
        start(remote(cin_ref.at[bt], call.at[a, b], c1s.at[k], c1r.at[b], column_device(a, bt)))
    for k, (org, other) in enumerate([(org, other) for org in others for other in range(2)] + [((0, 0), 1)]):
        at = cpos(*org, other)
        start(remote(lin_ref.at[pl.ds(pl.multiple_of(at * IB, IB), IB)], lraw.at[a], l1s.at[k], l1r.at[a], column_device(at, b)))
    call[a, b] = cin_ref[b]
    lraw[a] = lin_ref[pl.ds(pl.multiple_of(a * IB, IB), IB), :]

    def chalf(p, h):
        return call.at[p] if h is None else call.at[p, pl.ds(4 * h, 4)]

    def lhalf(p, h):
        return lpk.at[p] if h is None else lpk.at[p, pl.ds(5 * h, 5 - h)]

    slot_c, slot_l = [0], [0]

    def csend(org, h, to, seen):
        ref = chalf(cpos(*org), h)
        start(remote(ref, ref, c2s.at[slot_c[0]], c2r.at[seen[0] * 4 + seen[1], h or 0], column_device(cpos(*to), b)))
        slot_c[0] += 1

    def lsend(org, h, to, seen):
        ref = lhalf(lpos(*org), h)
        start(remote(ref, ref, l2s.at[slot_l[0]], l2r.at[seen[0] * 4 + seen[1], h or 0], column_device(a, lpos(*to))))
        slot_l[0] += 1

    def over(org, h=None):
        ref = chalf(cpos(*org), h)
        n = org[0] * 4 + org[1]
        start(remote(ref, ref, c3s.at[n, h or 0], c3r.at[n, h or 0], partner))

    def cwait(org, h=None):
        arrived(chalf(cpos(*org), h), c2r.at[org[0] * 4 + org[1], h or 0])

    def owait(org, h=None):
        arrived(chalf(cpos(*org, 1), h), c3r.at[org[0] * 4 + org[1], h or 0])

    def lwait(org, h=None):
        arrived(lhalf(lpos(*org), h), l2r.at[org[0] * 4 + org[1], h or 0])

    HERE, PAIR, UP, DOWN = (0, 0), (1, 0), (0, 1), (0, 3)
    left_lane = lax.broadcasted_iota(jnp.int32, (IB, LANES), 1)

    def unpack(org):
        bs = lpos(*org)
        for n in range(16):
            t, o = (n * ROWS2) // LANES, (n * ROWS2) % LANES
            tile = lpk[bs, t].astype(F32)
            if o:
                tile = pltpu.roll(tile, LANES - o, 1)
                if LANES - o < ROWS2:
                    tile = jnp.where(left_lane < LANES - o, tile, pltpu.roll(lpk[bs, t + 1].astype(F32), LANES - o, 1))
            lall[bs, n] = tile.astype(BF)

    for k in range(1, 8):
        bs = (b + 8 - k) % 8
        arrived(call.at[a, bs], c1r.at[bs])
    csend(HERE, None, PAIR, (1, 0))
    csend(HERE, None, UP, (0, 3))
    csend(HERE, None, DOWN, (0, 1))
    over(HERE)

    for k in range(1, 16):
        asrc = (a + 16 - k) % 16
        arrived(lraw.at[asrc], l1r.at[asrc])
    packed = jnp.concatenate([lraw[s][:, :ROWS2] for s in range(16)], axis=1)
    for t in range(9):
        lpk[b, t] = packed[:, t * LANES:(t + 1) * LANES]
    lsend(HERE, None, PAIR, (1, 0))
    lsend(HERE, None, UP, (0, 3))
    lsend(HERE, None, DOWN, (0, 1))

    cwait(PAIR)
    csend(PAIR, 1, UP, (1, 3))
    csend(PAIR, 1, DOWN, (1, 1))
    over(PAIR)
    lwait(PAIR)
    lsend(PAIR, 1, UP, (1, 3))
    lsend(PAIR, 1, DOWN, (1, 1))
    lall[b] = lraw[...]
    unpack(PAIR)
    cwait((0, 3))
    csend((0, 3), 0, UP, (0, 2))
    csend((0, 3), 0, PAIR, (1, 3))
    over((0, 3))
    cwait((0, 1))
    csend((0, 1), 1, DOWN, (0, 2))
    csend((0, 1), 0, PAIR, (1, 1))
    over((0, 1))
    lwait((0, 3))
    lsend((0, 3), 0, UP, (0, 2))
    lsend((0, 3), 0, PAIR, (1, 3))
    lwait((0, 1))
    lsend((0, 1), 1, DOWN, (0, 2))
    lsend((0, 1), 0, PAIR, (1, 1))
    unpack((0, 3))
    unpack((0, 1))
    for org, h, to in (((1, 3), 0, UP), ((1, 1), 1, DOWN)):
        cwait(org, h)
        csend(org, h, to, (1, 2))
        over(org, h)
        lwait(org, h)
        lsend(org, h, to, (1, 2))
    for org, h in (((1, 3), 1), ((1, 1), 0)):
        cwait(org, h)
        over(org, h)
        lwait(org, h)
    unpack((1, 3))
    unpack((1, 1))

    lane = lax.broadcasted_iota(jnp.int32, (IB, LANES), 1)
    first = jnp.where((lane % 2 == 0) & (lane < ROWS2), 1.0, 0.0).astype(BF)
    second = jnp.where((lane % 2 == 1) & (lane < ROWS2), 1.0, 0.0).astype(BF)
    lane1 = lax.broadcasted_iota(jnp.int32, (1, LANES), 1)
    scale = jnp.where(lane1 < JB, 1.0 / math.sqrt(TOKS), 0.0)

    def rows_of(other, rc, lsteps):
        asrc = cpos(*rel(rc), other)
        for rl in lsteps:
            bs = lpos(*rel(rl))
            left = lall[bs, asrc]
            left = jnp.concatenate([left * first, left * second], axis=0)
            right = call[asrc, bs]
            prod = lax.dot_general(left[:, :ROWS2], right, (((1,), (0,)), ((), ())), preferred_element_type=F32)
            at = asrc * 8 + flip(bs, asrc // 8)
            rbuf[pl.ds(pl.multiple_of(at * 2 * IB, 2 * IB), 2 * IB), :] = (prod * scale).astype(BF).astype(F32)
            esc[pl.ds(at, 1), :] = right.astype(F32)[0:1, :]

    def rows_loop(other, lo, hi, lsteps):
        def body(rc, carry):
            rows_of(other, rc, lsteps)
            return carry
        lax.fori_loop(lo, hi, body, 0)

    rows_loop(0, 0, 6, range(6))
    for org in (HERE, PAIR, DOWN, UP):
        owait(org)
    for org, h in (((1, 3), 0), ((1, 1), 1), ((1, 3), 1), ((1, 1), 0)):
        owait(org, h)
    rows_loop(1, 0, 6, range(6))
    for u in range(2):
        for h in range(2):
            cwait((u, 2), h)
            over((u, 2), h)
        for h in range(2):
            lwait((u, 2), h)
        unpack((u, 2))
    for other in range(2):
        rows_loop(other, 0, 6, range(6, 8))
    rows_loop(0, 6, 8, range(8))
    for u in range(2):
        for h in range(2):
            owait((u, 2), h)
    rows_loop(1, 6, 8, range(8))

    gacc[...] = jnp.zeros_like(gacc)
    inv_root = 1.0 / math.sqrt(WIDTH * WIDTH)

    def gram_step(m, carry):
        xs = [rbuf[pl.ds(pl.multiple_of(s * IB + m * 8, 8), 8), :] for s in range(SLOTS)]
        sums = xs[:8]
        for s in range(8, SLOTS):
            sums[s % 8] = sums[s % 8] + xs[s]
        while len(sums) > 1:
            sums = [sums[n] + sums[n + 1] for n in range(0, len(sums), 2)]
        mean = sums[0] * (1.0 / SLOTS)
        c = jnp.concatenate([((x - mean) * inv_root)[None] for x in xs], axis=0)
        c = jnp.transpose(c, (1, 0, 2)).astype(BF)
        cen_ref[pl.ds(pl.multiple_of(m * 8, 8), 8)] = c
        c = jnp.concatenate([c[n] for n in range(8)], axis=1)
        gacc[...] += lax.dot_general(c, c, (((1,), (1,)), ((), ())), preferred_element_type=F32)
        return carry

    lax.fori_loop(0, IB // 8, gram_step, 0)

    for t in range(48):
        blk, w = t // 16, t % 16
        r0 = (0, 128, 128)[blk] + 8 * w
        c0 = (0, 0, 128)[blk]
        gp[t // 24, (t % 24) // 3, t % 3] = gacc[r0:r0 + 8, c0:c0 + 128]

    start(remote(gp.at[1 - core], cbuf, a_s, a_r, partner))
    arrived(cbuf, a_r)
    cbuf[...] = cbuf[...] + gp[core]
    for k, org in enumerate(others):
        bt = lpos(*org)
        start(remote(cbuf.at[bt], rr.at[b], b_s.at[k], b_r.at[b], column_device(a, bt)))
    rr[b] = cbuf[b]

    parts = esc[...]
    pos = lax.broadcasted_iota(jnp.int32, (LANES, LANES), 0) * 2
    for half in range(2):
        row = jnp.zeros((1, LANES), F32)
        for k in range(2):
            e = parts[:, JB + 3 * k:JB + 3 * k + 1] + parts[:, JB + 3 * k + 1:JB + 3 * k + 2] + parts[:, JB + 3 * k + 2:JB + 3 * k + 3]
            hit = slot_ref[half:half + 1, :] == pos + k
            row = row + jnp.sum(jnp.where(hit, e, 0.0), axis=0, keepdims=True)
        erow_ref[half:half + 1, :] = row

    e_row = jnp.concatenate([erow_ref[0:1, :], erow_ref[1:2, :]], axis=1)
    sh = e_row - jnp.sum(e_row, axis=1, keepdims=True) * (1.0 / SLOTS)
    rows = lax.broadcasted_iota(jnp.int32, (SLOTS, SLOTS), 0)
    cols = lax.broadcasted_iota(jnp.int32, (SLOTS, SLOTS), 1)
    eye = rows == cols
    W[:, SLOTS:] = jnp.broadcast_to(jnp.sum(jnp.where(eye, sh, 0.0), axis=1, keepdims=True), (SLOTS, LANES))

    for k in range(1, 8):
        bs = (b + 8 - k) % 8
        arrived(rr.at[bs], b_r.at[bs])
    total = rr[0]
    for k in range(1, 8):
        total = total + rr[k]
    s1[...] = total
    chip = x_hi * 4 + z
    cr[chip] = total
    for k, org in enumerate(others):
        start(remote(s1, cr.at[chip], x_s.at[k], x_r.at[chip], column_device(cpos(*org), b)))
    for k in range(1, 8):
        cs = (chip + 8 - k) % 8
        arrived(cr.at[cs], x_r.at[cs])
    total = cr[0]
    for k in range(1, 8):
        total = total + cr[k]
    s2[...] = total
    gt[core, b] = total
    for k, org in enumerate(others):
        start(remote(s2, gt.at[core, b], d_s.at[k], d_r.at[b], column_device(a, lpos(*org))))
        start(remote(s2, gt.at[core, b], e_s.at[k + 1], e_r.at[b], column_device(a + across, lpos(*org))))
    start(remote(s2, gt.at[core, b], e_s.at[0], e_r.at[b], partner))
    for k in range(1, 8):
        bs = (b + 8 - k) % 8
        arrived(gt.at[core, bs], d_r.at[bs])
    for k in range(8):
        bs = (b + 8 - k) % 8
        arrived(gt.at[1 - core, bs], e_r.at[bs])

    for t in range(48):
        blk, w = t // 16, t % 16
        r0 = (0, 128, 128)[blk] + 8 * w
        c0 = (0, 0, 128)[blk]
        W[r0:r0 + 8, c0:c0 + 128] = gt[t // 24, (t % 24) // 3, t % 3]
    W[0:128, 128:256] = W[128:256, 0:128].T
    W[:, 0:SLOTS] = W[:, 0:SLOTS] + jnp.where(eye, damp_ref[0], 0.0)
    weights, last = sweep(W, SLOTS, 8)
    wv[...] = weights
    wv[SLOTS - 8:, :] = last

    def update_rows(r):
        done = []
        for v in range(6):
            c = cen_ref[r * 6 + v].astype(F32)
            done.append(jnp.sum(c * wv[...], axis=0, keepdims=True))
        done.append(jnp.zeros((2, LANES), F32))
        upd[r] = jnp.concatenate(done, axis=0)

    for k, org in enumerate(others):
        bt = lpos(*org)
        update_rows(flip(bt, x_hi))
        start(remote(upd.at[flip(bt, x_hi)], ur.at[b], f_s.at[k], f_r.at[b], column_device(a, bt)))
    update_rows(rb)
    ur[b] = upd[rb]
    for copy in sends[:-7]:
        copy.wait_send()
    for k in range(1, 8):
        bs = (b + 8 - k) % 8
        arrived(ur.at[bs], f_r.at[bs])
    whole = jnp.concatenate([ur[n][:, :JB] for n in range(8)], axis=1)
    for i in range(6):
        for v in range(6):
            out_ref[6 * i + v:6 * i + v + 1, :] = whole[i:i + 1, v * LANES:(v + 1) * LANES]
    for copy in sends[-7:]:
        copy.wait_send()


def main_call(energies, damping, spin, acts, cot, embed, slots):
    dma = pltpu.SemaphoreType.DMA
    smem = pl.BlockSpec(memory_space=pltpu.SMEM)
    hbm = pl.BlockSpec(memory_space=pl.ANY)
    return pl.pallas_call(
        main_kernel,
        out_shape=jax.ShapeDtypeStruct((36, LANES), F32),
        in_specs=[smem, smem, hbm, hbm, hbm, hbm, hbm],
        out_specs=pl.BlockSpec(memory_space=pltpu.VMEM),
        scratch_shapes=[
            pltpu.VMEM(spin.shape, jnp.int32),
            pltpu.VMEM(acts.shape, BF),
            pltpu.VMEM(cot.shape, BF),
            pltpu.VMEM(embed.shape, BF),
            pltpu.VMEM(slots.shape, jnp.int32),
            dma((5,)),
            pltpu.VMEM((LANES, WIDTH), F32),
            pltpu.VMEM((ROWS2, WIDTH), F32),
            pltpu.VMEM((WIDTH, LANES), BF),
            pltpu.VMEM((8, ROWS2, LANES), BF),
            pltpu.VMEM((2, 8, 3, 8, LANES), F32),
            pltpu.VMEM((2, LANES), F32),
            pltpu.VMEM((IB, SLOTS, LANES), BF),
            pltpu.VMEM((SLOTS, SLOTS + LANES), F32),
            pltpu.VMEM((SLOTS, LANES), F32),
            pltpu.VMEM((8, 8, LANES), F32),
            pltpu.VMEM((8, 8, LANES), F32),
            dma((8,)), dma((8,)),
            pltpu.VMEM((16, IB, LANES), BF),
            pltpu.VMEM((8, 9, IB, LANES), BF),
            pltpu.VMEM((8, 16, IB, LANES), BF),
            pltpu.VMEM((16, 8, ROWS2, LANES), BF),
            pltpu.VMEM((SLOTS * IB, LANES), F32),
            pltpu.VMEM((LANES, LANES), F32),
            pltpu.VMEM((SLOTS, SLOTS), F32),
            pltpu.VMEM((2, 8, 3, 8, LANES), F32),
            pltpu.VMEM((8, 3, 8, LANES), F32),
            pltpu.VMEM((8, 3, 8, LANES), F32),
            pltpu.VMEM((3, 8, LANES), F32),
            pltpu.VMEM((8, 3, 8, LANES), F32),
            pltpu.VMEM((3, 8, LANES), F32),
            dma((16,)), dma((16,)), dma((8,)), dma((8,)), dma((11,)), dma((8, 2)),
            dma((8, 2)), dma((8, 2)), dma((11,)), dma((8, 2)),
            dma(()), dma(()), dma((8,)), dma((8,)), dma((8,)), dma((8,)), dma((8,)), dma((8,)), dma((8,)), dma((8,)),
        ],
        compiler_params=pltpu.CompilerParams(
            collective_id=0, has_side_effects=True, vmem_limit_bytes=60000000),
        name="main",
    )(energies, damping, spin, acts, cot, embed, slots)


def shards(spin_config, layer_acts, cotangent, patch_embed, energies, slot_sample, damping):
    out = main_call(energies, damping.reshape(1), spin_config, layer_acts.transpose(1, 0, 2),
                    cotangent.transpose(1, 0, 2), patch_embed,
                    slot_sample.reshape(2, LANES))
    return (out * -math.sqrt(WIDTH * WIDTH / SLOTS)).reshape(-1)


def solution(mesh):
    return jax.shard_map(
        shards,
        mesh=mesh,
        in_specs=(
            P(("grp", "dev"), None),
            P(("grp", "dev"), None, None),
            P(("grp", "dev"), None, None),
            P(),
            P(("grp", "dev")),
            P(),
            P(),
        ),
        out_specs=P(("grp", "dev")),
        check_vma=False,
    )
```

```python
import math

import jax
import jax.numpy as jnp
from jax import lax
from jax.experimental import pallas as pl
from jax.experimental.pallas import tpu as pltpu
from jax.sharding import PartitionSpec as P

F32 = jnp.float32
BF = jnp.bfloat16
MESH = pl.DeviceIdType.MESH
SLOTS = 256
WIDTH = 768
SITES = 144
PATCH = 4
TOKS = 36
IB = 48
JB = 96
ROWS2 = 2 * TOKS
LANES = 128


def flip(index, high):
    return index + high * (1 - 2 * (index % 2))


def place():
    g = lax.axis_index("grp")
    d = lax.axis_index("dev")
    x_hi, core = g // 2, g % 2
    z, rb = d // 8, d % 8
    return g, d, x_hi, core, z, rb


def column_device(a, b):
    g, z = a // 4, a % 4
    return (g, z * 8 + flip(b, g // 2))


def remote(src, dst, send_sem, recv_sem, device):
    return pltpu.make_async_remote_copy(
        src_ref=src, dst_ref=dst, send_sem=send_sem, recv_sem=recv_sem,
        device_id=device, device_id_type=MESH,
    )


def rel(r):
    m = r // 2
    return r % 2, m + (m // 2) * (1 - 2 * (m % 2))


def split3(x):
    high = x.astype(BF)
    rest = x - high.astype(F32)
    mid = rest.astype(BF)
    return high, mid, (rest - mid.astype(F32)).astype(BF)


def recip(x):
    r = pl.reciprocal(x, approx=True)
    return r * (2.0 - x * r)


def sweep(W, n, B):
    sub = lax.broadcasted_iota(jnp.int32, (B, LANES), 0)
    lane = lax.broadcasted_iota(jnp.int32, (B, LANES), 1)
    masks = [sub == i for i in range(B)]
    T = n // LANES

    def chain(k, p):
        t0, l0 = (B * k) // LANES, (B * k) % LANES
        c = [jnp.broadcast_to(p[t0][:, l0 + j:l0 + j + 1], (B, LANES)) for j in range(B)]
        p = list(p)
        for i in range(B):
            inv = recip(c[i][i:i + 1, :])
            ci = c[i]
            for j in range(B):
                if j == i:
                    c[j] = jnp.where(masks[i], inv, -ci * inv)
                else:
                    t = c[j][i:i + 1, :] * inv
                    c[j] = jnp.where(masks[i], t, c[j] - ci * t)
            for v in range(T + 1):
                r = p[v][i:i + 1, :] * inv
                p[v] = jnp.where(masks[i], r, p[v] - ci * r)
        dinv = jnp.zeros((B, LANES), F32)
        for j in range(B):
            dinv = jnp.where(lane == l0 + j, c[j], dinv)
        inside = (lane >= l0) & (lane < l0 + B)
        ident = jnp.where(lane == l0 + sub, 1.0, 0.0)
        x = list(p)
        x[t0] = jnp.where(inside, ident - dinv, p[t0])
        return x, p[T]

    def stack(p, x):
        ph, pm, pl_ = split3(p)
        xh, xm, xl = split3(x)
        join = lambda *parts: jnp.concatenate([q.astype(F32) for q in parts], axis=0).astype(BF)
        return join(ph, ph, pm, ph, pl_, pm), join(xh, xm, xh, xl, xh, xm)

    cat = lambda v: jnp.concatenate(v, axis=1)
    tn = (((0,), (0,)), ((), ()))
    p = [W[0:B, v * LANES:(v + 1) * LANES] for v in range(T + 1)]
    old = None
    for k in range(n // B):
        if old is not None:
            po, xo, xso = old
            ps, xs = stack(cat(po[:T]), cat(xo))
            r0 = B * (k + 1)
            m0 = LANES if r0 >= LANES else 0
            if r0 < n:
                change = lax.dot_general(ps[:, m0:], xs[:, :n], tn, preferred_element_type=F32)
                W[r0:, :n] = W[r0:, :n] - change[r0 - m0:, :]
            W[:, n:] = W[:, n:] - lax.dot_general(ps, xs[:, n:], tn, preferred_element_type=F32)
            W[B * (k - 1):B * k, n:] = xso
        x, xs = chain(k, p)
        old = (p, x, xs)
        if k + 1 < n // B:
            nxt = [W[B * (k + 1):B * (k + 2), v * LANES:(v + 1) * LANES] for v in range(T + 1)]
            t0, l0 = (B * k) // LANES, (B * k) % LANES
            cols = [nxt[t0][:, l0 + i:l0 + i + 1] for i in range(B)]
            for v in range(T + 1):
                terms = [cols[i] * x[v][i:i + 1, :] for i in range(B)]
                while len(terms) > 1:
                    terms = [terms[q] + terms[q + 1] for q in range(0, len(terms), 2)]
                nxt[v] = nxt[v] - terms[0]
            p = nxt
    po, xo, xso = old
    ps, xs = stack(cat(po[:T]), xo[T])
    return W[:, n:] - lax.dot_general(ps, xs, tn, preferred_element_type=F32), xso


def prepare(spin, acts, cot, embed, energy_ref, stage, cstage, lin, cin):
    for t in range(TOKS):
        stage[2 * t:2 * t + 2, :] = acts[t].astype(F32)
        cstage[2 * t:2 * t + 2, :] = cot[t].astype(F32)
    sub = lax.broadcasted_iota(jnp.int32, (ROWS2, SITES), 0)
    site = lax.broadcasted_iota(jnp.int32, (ROWS2, SITES), 1)
    spins = spin[...].astype(F32)
    patches = jnp.where(sub % 2 == 0, spins[0:1, :], spins[1:2, :])
    patches = jnp.where(site // PATCH == sub // 2, patches, 0.0).astype(BF)
    turn = lax.broadcasted_iota(jnp.int32, (SITES, WIDTH), 0) % PATCH
    table = embed[...].astype(F32)
    spread = jnp.zeros((SITES, WIDTH), F32)
    for k in range(PATCH):
        spread = jnp.where(turn == k, table[k:k + 1, :], spread)
    added = jnp.dot(patches, spread.astype(BF), preferred_element_type=F32)
    stage[:ROWS2, :] = (stage[:ROWS2, :] + added).astype(BF).astype(F32)
    stage[ROWS2:, :] = jnp.zeros((LANES - ROWS2, WIDTH), F32)
    for v in range(WIDTH // LANES):
        lin[v * LANES:(v + 1) * LANES, :] = stage[:, v * LANES:(v + 1) * LANES].T.astype(BF)
    lane = lax.broadcasted_iota(jnp.int32, (ROWS2, LANES), 1)
    row = lax.broadcasted_iota(jnp.int32, (ROWS2, LANES), 0)
    energy = jnp.where(lane < JB + 3, jnp.full((ROWS2, LANES), energy_ref[0], F32), jnp.full((ROWS2, LANES), energy_ref[1], F32))
    high, mid, low = (t.astype(F32) for t in split3(energy))
    third = lane % 3
    parts = jnp.where(third == 0, high, jnp.where(third == 1, mid, low))
    parts = jnp.where((row == 0) & (lane < JB + 6), parts, 0.0)
    for b in range(8):
        t, o = (JB * b) // LANES, (JB * b) % LANES
        piece = cstage[:, t * LANES:(t + 1) * LANES]
        if o:
            piece = pltpu.roll(piece, LANES - o, 1)
            if LANES - o < JB:
                after = pltpu.roll(cstage[:, (t + 1) * LANES:(t + 2) * LANES], LANES - o, 1)
                piece = jnp.where(lane < LANES - o, piece, after)
        cin[b] = jnp.where(lane < JB, piece, parts).astype(BF)


def main_kernel(energy_ref, damp_ref, spin_hbm, acts_hbm, cot_hbm, embed_hbm, slot_hbm, out_ref,
                spin_v, acts_v, cot_v, embed_v, slot_ref, in_sem, stage, cstage, lin_ref, cin_ref,
                gt, erow_ref, cen_ref, W, wv, upd, ur, f_s, f_r,
                lraw, lpk, lall, call, rbuf, esc, gacc, gp, cbuf, rr, s1, cr, s2,
                l1s, l1r, c1s, c1r, c2s, c2r, c3s, c3r, l2s, l2r,
                a_s, a_r, b_s, b_r, x_s, x_r, d_s, d_r, e_s, e_r):
    g, d, x_hi, core, z, rb = place()
    a = g * 4 + z
    b = flip(rb, x_hi)
    q, y = b % 2, b // 2
    partner = (x_hi * 2 + 1 - core, d)

    def cpos(du, dv, other=0):
        c = core + other * (1 - 2 * core)
        return (((x_hi + du) % 2) * 2 + c) * 4 + (z + dv) % 4

    def lpos(du, dv):
        return ((y + dv) % 4) * 2 + (q + du) % 2

    barrier = pltpu.get_barrier_semaphore()
    for k in range(1, 16):
        pl.semaphore_signal(barrier, inc=1, device_id=column_device((a + k) % 16, b), device_id_type=MESH)
    for k in range(1, 8):
        pl.semaphore_signal(barrier, inc=1, device_id=column_device(a, (b + k) % 8), device_id_type=MESH)
    across = (1 - 2 * core) * 4
    for k in range(1, 8):
        pl.semaphore_signal(barrier, inc=1, device_id=column_device(a + across, (b + k) % 8), device_id_type=MESH)
    loads = [pltpu.make_async_copy(src, dst, in_sem.at[n]) for n, (src, dst) in enumerate(
        ((spin_hbm, spin_v), (acts_hbm, acts_v), (cot_hbm, cot_v), (embed_hbm, embed_v), (slot_hbm, slot_ref)))]
    for copy in loads:
        copy.start()
    for copy in loads:
        copy.wait()
    prepare(spin_v, acts_v, cot_v, embed_v, energy_ref, stage, cstage, lin_ref, cin_ref)
    pl.semaphore_wait(barrier, 29)

    sends = []

    def start(copy):
        copy.start()
        sends.append(copy)

    def arrived(ref, sem):
        remote(ref, ref, sem, sem, partner).wait_recv()

    others = ((1, 2), (0, 2), (1, 1), (1, 3), (0, 1), (0, 3), (1, 0))
    for k, org in enumerate(others):
        bt = lpos(*org)
        start(remote(cin_ref.at[bt], call.at[a, b], c1s.at[k], c1r.at[b], column_device(a, bt)))
    for k, (org, other) in enumerate([(org, other) for org in others for other in range(2)] + [((0, 0), 1)]):
        at = cpos(*org, other)
        start(remote(lin_ref.at[pl.ds(pl.multiple_of(at * IB, IB), IB)], lraw.at[a], l1s.at[k], l1r.at[a], column_device(at, b)))
    call[a, b] = cin_ref[b]
    lraw[a] = lin_ref[pl.ds(pl.multiple_of(a * IB, IB), IB), :]

    def chalf(p, h):
        return call.at[p] if h is None else call.at[p, pl.ds(4 * h, 4)]

    def lhalf(p, h):
        return lpk.at[p] if h is None else lpk.at[p, pl.ds(5 * h, 5 - h)]

    slot_c, slot_l = [0], [0]

    def csend(org, h, to, seen):
        ref = chalf(cpos(*org), h)
        start(remote(ref, ref, c2s.at[slot_c[0]], c2r.at[seen[0] * 4 + seen[1], h or 0], column_device(cpos(*to), b)))
        slot_c[0] += 1

    def lsend(org, h, to, seen):
        ref = lhalf(lpos(*org), h)
        start(remote(ref, ref, l2s.at[slot_l[0]], l2r.at[seen[0] * 4 + seen[1], h or 0], column_device(a, lpos(*to))))
        slot_l[0] += 1

    def over(org, h=None):
        ref = chalf(cpos(*org), h)
        n = org[0] * 4 + org[1]
        start(remote(ref, ref, c3s.at[n, h or 0], c3r.at[n, h or 0], partner))

    def cwait(org, h=None):
        arrived(chalf(cpos(*org), h), c2r.at[org[0] * 4 + org[1], h or 0])

    def owait(org, h=None):
        arrived(chalf(cpos(*org, 1), h), c3r.at[org[0] * 4 + org[1], h or 0])

    def lwait(org, h=None):
        arrived(lhalf(lpos(*org), h), l2r.at[org[0] * 4 + org[1], h or 0])

    HERE, PAIR, UP, DOWN = (0, 0), (1, 0), (0, 1), (0, 3)
    left_lane = lax.broadcasted_iota(jnp.int32, (IB, LANES), 1)

    def unpack(org):
        bs = lpos(*org)
        for n in range(16):
            t, o = (n * ROWS2) // LANES, (n * ROWS2) % LANES
            tile = lpk[bs, t].astype(F32)
            if o:
                tile = pltpu.roll(tile, LANES - o, 1)
                if LANES - o < ROWS2:
                    tile = jnp.where(left_lane < LANES - o, tile, pltpu.roll(lpk[bs, t + 1].astype(F32), LANES - o, 1))
            lall[bs, n] = tile.astype(BF)

    for k in range(1, 8):
        bs = (b + 8 - k) % 8
        arrived(call.at[a, bs], c1r.at[bs])
    csend(HERE, None, PAIR, (1, 0))
    csend(HERE, None, UP, (0, 3))
    csend(HERE, None, DOWN, (0, 1))
    over(HERE)

    for k in range(1, 16):
        asrc = (a + 16 - k) % 16
        arrived(lraw.at[asrc], l1r.at[asrc])
    packed = jnp.concatenate([lraw[s][:, :ROWS2] for s in range(16)], axis=1)
    for t in range(9):
        lpk[b, t] = packed[:, t * LANES:(t + 1) * LANES]
    lsend(HERE, None, PAIR, (1, 0))
    lsend(HERE, None, UP, (0, 3))
    lsend(HERE, None, DOWN, (0, 1))

    cwait(PAIR)
    csend(PAIR, 1, UP, (1, 3))
    csend(PAIR, 1, DOWN, (1, 1))
    over(PAIR)
    lwait(PAIR)
    lsend(PAIR, 1, UP, (1, 3))
    lsend(PAIR, 1, DOWN, (1, 1))
    lall[b] = lraw[...]
    unpack(PAIR)
    cwait((0, 3))
    csend((0, 3), 0, UP, (0, 2))
    csend((0, 3), 0, PAIR, (1, 3))
    over((0, 3))
    cwait((0, 1))
    csend((0, 1), 1, DOWN, (0, 2))
    csend((0, 1), 0, PAIR, (1, 1))
    over((0, 1))
    lwait((0, 3))
    lsend((0, 3), 0, UP, (0, 2))
    lsend((0, 3), 0, PAIR, (1, 3))
    lwait((0, 1))
    lsend((0, 1), 1, DOWN, (0, 2))
    lsend((0, 1), 0, PAIR, (1, 1))
    unpack((0, 3))
    unpack((0, 1))
    for org, h, to in (((1, 3), 0, UP), ((1, 1), 1, DOWN)):
        cwait(org, h)
        csend(org, h, to, (1, 2))
        over(org, h)
        lwait(org, h)
        lsend(org, h, to, (1, 2))
    for org, h in (((1, 3), 1), ((1, 1), 0)):
        cwait(org, h)
        over(org, h)
        lwait(org, h)
    unpack((1, 3))
    unpack((1, 1))

    lane = lax.broadcasted_iota(jnp.int32, (IB, LANES), 1)
    first = jnp.where((lane % 2 == 0) & (lane < ROWS2), 1.0, 0.0).astype(BF)
    second = jnp.where((lane % 2 == 1) & (lane < ROWS2), 1.0, 0.0).astype(BF)
    lane1 = lax.broadcasted_iota(jnp.int32, (1, LANES), 1)
    scale = jnp.where(lane1 < JB, 1.0 / math.sqrt(TOKS), 0.0)

    def rows_of(other, rc, lsteps):
        asrc = cpos(*rel(rc), other)
        for rl in lsteps:
            bs = lpos(*rel(rl))
            left = lall[bs, asrc]
            left = jnp.concatenate([left * first, left * second], axis=0)
            right = call[asrc, bs]
            prod = lax.dot_general(left[:, :ROWS2], right, (((1,), (0,)), ((), ())), preferred_element_type=F32)
            at = asrc * 8 + flip(bs, asrc // 8)
            rbuf[pl.ds(pl.multiple_of(at * 2 * IB, 2 * IB), 2 * IB), :] = (prod * scale).astype(BF).astype(F32)
            esc[pl.ds(at, 1), :] = right.astype(F32)[0:1, :]

    def rows_loop(other, lo, hi, lsteps):
        def body(rc, carry):
            rows_of(other, rc, lsteps)
            return carry
        lax.fori_loop(lo, hi, body, 0, unroll=2)

    rows_loop(0, 0, 6, range(6))
    for org in (HERE, PAIR, DOWN, UP):
        owait(org)
    for org, h in (((1, 3), 0), ((1, 1), 1), ((1, 3), 1), ((1, 1), 0)):
        owait(org, h)
    rows_loop(1, 0, 6, range(6))
    for u in range(2):
        for h in range(2):
            cwait((u, 2), h)
            over((u, 2), h)
        for h in range(2):
            lwait((u, 2), h)
        unpack((u, 2))
    for other in range(2):
        rows_loop(other, 0, 6, range(6, 8))
    rows_loop(0, 6, 8, range(8))
    for u in range(2):
        for h in range(2):
            owait((u, 2), h)
    rows_loop(1, 6, 8, range(8))

    gacc[...] = jnp.zeros_like(gacc)
    inv_root = 1.0 / math.sqrt(WIDTH * WIDTH)

    def gram_step(m, carry):
        xs = [rbuf[pl.ds(pl.multiple_of(s * IB + m * 8, 8), 8), :] for s in range(SLOTS)]
        sums = xs[:8]
        for s in range(8, SLOTS):
            sums[s % 8] = sums[s % 8] + xs[s]
        while len(sums) > 1:
            sums = [sums[n] + sums[n + 1] for n in range(0, len(sums), 2)]
        mean = sums[0] * (1.0 / SLOTS)
        c = jnp.concatenate([((x - mean) * inv_root)[None] for x in xs], axis=0)
        c = jnp.transpose(c, (1, 0, 2)).astype(BF)
        cen_ref[pl.ds(pl.multiple_of(m * 8, 8), 8)] = c
        c = jnp.concatenate([c[n] for n in range(8)], axis=1)
        gacc[...] += lax.dot_general(c, c, (((1,), (1,)), ((), ())), preferred_element_type=F32)
        return carry

    lax.fori_loop(0, IB // 8, gram_step, 0, unroll=2)

    for t in range(48):
        blk, w = t // 16, t % 16
        r0 = (0, 128, 128)[blk] + 8 * w
        c0 = (0, 0, 128)[blk]
        gp[t // 24, (t % 24) // 3, t % 3] = gacc[r0:r0 + 8, c0:c0 + 128]

    start(remote(gp.at[1 - core], cbuf, a_s, a_r, partner))
    arrived(cbuf, a_r)
    cbuf[...] = cbuf[...] + gp[core]
    for k, org in enumerate(others):
        bt = lpos(*org)
        start(remote(cbuf.at[bt], rr.at[b], b_s.at[k], b_r.at[b], column_device(a, bt)))
    rr[b] = cbuf[b]

    parts = esc[...]
    pos = lax.broadcasted_iota(jnp.int32, (LANES, LANES), 0) * 2
    for half in range(2):
        row = jnp.zeros((1, LANES), F32)
        for k in range(2):
            e = parts[:, JB + 3 * k:JB + 3 * k + 1] + parts[:, JB + 3 * k + 1:JB + 3 * k + 2] + parts[:, JB + 3 * k + 2:JB + 3 * k + 3]
            hit = slot_ref[half:half + 1, :] == pos + k
            row = row + jnp.sum(jnp.where(hit, e, 0.0), axis=0, keepdims=True)
        erow_ref[half:half + 1, :] = row

    e_row = jnp.concatenate([erow_ref[0:1, :], erow_ref[1:2, :]], axis=1)
    sh = e_row - jnp.sum(e_row, axis=1, keepdims=True) * (1.0 / SLOTS)
    rows = lax.broadcasted_iota(jnp.int32, (SLOTS, SLOTS), 0)
    cols = lax.broadcasted_iota(jnp.int32, (SLOTS, SLOTS), 1)
    eye = rows == cols
    W[:, SLOTS:] = jnp.broadcast_to(jnp.sum(jnp.where(eye, sh, 0.0), axis=1, keepdims=True), (SLOTS, LANES))

    for k in range(1, 8):
        bs = (b + 8 - k) % 8
        arrived(rr.at[bs], b_r.at[bs])
    total = rr[0]
    for k in range(1, 8):
        total = total + rr[k]
    s1[...] = total
    chip = x_hi * 4 + z
    cr[chip] = total
    for k, org in enumerate(others):
        start(remote(s1, cr.at[chip], x_s.at[k], x_r.at[chip], column_device(cpos(*org), b)))
    for k in range(1, 8):
        cs = (chip + 8 - k) % 8
        arrived(cr.at[cs], x_r.at[cs])
    total = cr[0]
    for k in range(1, 8):
        total = total + cr[k]
    s2[...] = total
    gt[core, b] = total
    for k, org in enumerate(others):
        start(remote(s2, gt.at[core, b], d_s.at[k], d_r.at[b], column_device(a, lpos(*org))))
        start(remote(s2, gt.at[core, b], e_s.at[k + 1], e_r.at[b], column_device(a + across, lpos(*org))))
    start(remote(s2, gt.at[core, b], e_s.at[0], e_r.at[b], partner))
    for k in range(1, 8):
        bs = (b + 8 - k) % 8
        arrived(gt.at[core, bs], d_r.at[bs])
    for k in range(8):
        bs = (b + 8 - k) % 8
        arrived(gt.at[1 - core, bs], e_r.at[bs])

    for t in range(48):
        blk, w = t // 16, t % 16
        r0 = (0, 128, 128)[blk] + 8 * w
        c0 = (0, 0, 128)[blk]
        W[r0:r0 + 8, c0:c0 + 128] = gt[t // 24, (t % 24) // 3, t % 3]
    W[0:128, 128:256] = W[128:256, 0:128].T
    W[:, 0:SLOTS] = W[:, 0:SLOTS] + jnp.where(eye, damp_ref[0], 0.0)
    weights, last = sweep(W, SLOTS, 8)
    wv[...] = weights
    wv[SLOTS - 8:, :] = last

    def update_rows(r):
        done = []
        for v in range(6):
            c = cen_ref[r * 6 + v].astype(F32)
            done.append(jnp.sum(c * wv[...], axis=0, keepdims=True))
        done.append(jnp.zeros((2, LANES), F32))
        upd[r] = jnp.concatenate(done, axis=0)

    for k, org in enumerate(others):
        bt = lpos(*org)
        update_rows(flip(bt, x_hi))
        start(remote(upd.at[flip(bt, x_hi)], ur.at[b], f_s.at[k], f_r.at[b], column_device(a, bt)))
    update_rows(rb)
    ur[b] = upd[rb]
    for copy in sends[:-7]:
        copy.wait_send()
    for k in range(1, 8):
        bs = (b + 8 - k) % 8
        arrived(ur.at[bs], f_r.at[bs])
    whole = jnp.concatenate([ur[n][:, :JB] for n in range(8)], axis=1)
    for i in range(6):
        for v in range(6):
            out_ref[6 * i + v:6 * i + v + 1, :] = whole[i:i + 1, v * LANES:(v + 1) * LANES]
    for copy in sends[-7:]:
        copy.wait_send()


def main_call(energies, damping, spin, acts, cot, embed, slots):
    dma = pltpu.SemaphoreType.DMA
    smem = pl.BlockSpec(memory_space=pltpu.SMEM)
    hbm = pl.BlockSpec(memory_space=pl.ANY)
    return pl.pallas_call(
        main_kernel,
        out_shape=jax.ShapeDtypeStruct((36, LANES), F32),
        in_specs=[smem, smem, hbm, hbm, hbm, hbm, hbm],
        out_specs=pl.BlockSpec(memory_space=pltpu.VMEM),
        scratch_shapes=[
            pltpu.VMEM(spin.shape, jnp.int32),
            pltpu.VMEM(acts.shape, BF),
            pltpu.VMEM(cot.shape, BF),
            pltpu.VMEM(embed.shape, BF),
            pltpu.VMEM(slots.shape, jnp.int32),
            dma((5,)),
            pltpu.VMEM((LANES, WIDTH), F32),
            pltpu.VMEM((ROWS2, WIDTH), F32),
            pltpu.VMEM((WIDTH, LANES), BF),
            pltpu.VMEM((8, ROWS2, LANES), BF),
            pltpu.VMEM((2, 8, 3, 8, LANES), F32),
            pltpu.VMEM((2, LANES), F32),
            pltpu.VMEM((IB, SLOTS, LANES), BF),
            pltpu.VMEM((SLOTS, SLOTS + LANES), F32),
            pltpu.VMEM((SLOTS, LANES), F32),
            pltpu.VMEM((8, 8, LANES), F32),
            pltpu.VMEM((8, 8, LANES), F32),
            dma((8,)), dma((8,)),
            pltpu.VMEM((16, IB, LANES), BF),
            pltpu.VMEM((8, 9, IB, LANES), BF),
            pltpu.VMEM((8, 16, IB, LANES), BF),
            pltpu.VMEM((16, 8, ROWS2, LANES), BF),
            pltpu.VMEM((SLOTS * IB, LANES), F32),
            pltpu.VMEM((LANES, LANES), F32),
            pltpu.VMEM((SLOTS, SLOTS), F32),
            pltpu.VMEM((2, 8, 3, 8, LANES), F32),
            pltpu.VMEM((8, 3, 8, LANES), F32),
            pltpu.VMEM((8, 3, 8, LANES), F32),
            pltpu.VMEM((3, 8, LANES), F32),
            pltpu.VMEM((8, 3, 8, LANES), F32),
            pltpu.VMEM((3, 8, LANES), F32),
            dma((16,)), dma((16,)), dma((8,)), dma((8,)), dma((11,)), dma((8, 2)),
            dma((8, 2)), dma((8, 2)), dma((11,)), dma((8, 2)),
            dma(()), dma(()), dma((8,)), dma((8,)), dma((8,)), dma((8,)), dma((8,)), dma((8,)), dma((8,)), dma((8,)),
        ],
        compiler_params=pltpu.CompilerParams(
            collective_id=0, has_side_effects=True, vmem_limit_bytes=60000000),
        name="main",
    )(energies, damping, spin, acts, cot, embed, slots)


def shards(spin_config, layer_acts, cotangent, patch_embed, energies, slot_sample, damping):
    out = main_call(energies, damping.reshape(1), spin_config, layer_acts.transpose(1, 0, 2),
                    cotangent.transpose(1, 0, 2), patch_embed,
                    slot_sample.reshape(2, LANES))
    return (out * -math.sqrt(WIDTH * WIDTH / SLOTS)).reshape(-1)


def solution(mesh):
    return jax.shard_map(
        shards,
        mesh=mesh,
        in_specs=(
            P(("grp", "dev"), None),
            P(("grp", "dev"), None, None),
            P(("grp", "dev"), None, None),
            P(),
            P(("grp", "dev")),
            P(),
            P(),
        ),
        out_specs=P(("grp", "dev")),
        check_vma=False,
    )
```
